128 devices in a mesh: table: 8 (over y, core), seq: 16 (over z, x).
Axes of the slice: x: 4, y: 4, z: 4, core: 2. Of those that a mesh axis runs over, the one named last changes fastest.
Arguments:
- item_ids: int32 [8, 4096], P('table', 'seq'), may hold values from 0 to 524287, as said below
- history_len: int32 [8], P('table'), may hold values from 1024 to 4096, as said below
- row_place: int32 [524288], replicated, may hold values from 0 to 524287, as said below
- item_table: bfloat16 [524288, 512], P(('table', 'seq')), may hold values from -6 to 6
- input_proj: bfloat16 [512, 2048], replicated, may hold values from -0.25 to 0.25
- output_proj: bfloat16 [512, 512], replicated, may hold values from -0.25 to 0.25
- out_cotangent: bfloat16 [8, 4096, 512], P('table', 'seq'), may hold values from -18 to 18
Outputs:
- layer_out: bfloat16 [8, 4096, 512], P('table', 'seq')
- table_grad: bfloat16 [524288, 512], P(('table', 'seq'))
The draws below stay inside these ranges and needn't reach their ends.
Inputs may be any that keep to these rules, and one draw needn't show every extreme that they name: `item_ids`: within the 256 positions of one device, at most 6 items are stored in any one owner's block of 4096 table rows (rows o * 4096 to (o + 1) * 4096 - 1); one owner's block receives exactly 6 from the positions of every device. `row_place`: A permutation: every table row holds exactly one item. `history_len`: at least one history fills all 4096 positions.
All inputs are finite; a program needn't handle non-finite values.
Results may differ from the reference program's by a relative error of at most 0.006.
Values may be sent and summed in bfloat16 or wider, within the bound.
A program may use at most 128 MiB of HBM per device.

```python
import math
import jax
import jax.numpy as jnp
from jax import lax

D = 512
HEADS = 8
HEAD_DIM = 64
LEN_DEV = 256
ROWS_DEV = 4096
USERS = 8
LENGTH = 4096
OWNERS = 128
VOCAB = 524288
CAP = 6


def make_rows(key):
    base_key = jax.random.fold_in(key, 11)
    storage = jax.random.permutation(jax.random.fold_in(base_key, 1), VOCAB).astype(jnp.int32)
    inverse = jnp.argsort(storage, stable=True).astype(jnp.int32)
    hot_owner = jax.random.randint(jax.random.fold_in(base_key, 2), (), 0, OWNERS)
    blocks_all = USERS * (LENGTH // LEN_DEV)
    block_keys = jax.random.split(jax.random.fold_in(base_key, 3), blocks_all)
    slot_total = OWNERS * CAP

    def one_block(block_key):
        key_a, key_b, key_c = jax.random.split(block_key, 3)
        slot_ids = jax.random.permutation(key_a, slot_total).astype(jnp.int32)
        owner_of = slot_ids // CAP
        slot_order = jnp.arange(slot_total, dtype=jnp.int32)
        slot_score = jnp.where(owner_of == hot_owner, slot_order - slot_total, slot_order)
        chosen = jnp.argsort(slot_score, stable=True)[:LEN_DEV]
        picked = owner_of[chosen]
        picked = picked[jax.random.permutation(key_b, LEN_DEV)]
        local_row = jax.random.randint(key_c, (LEN_DEV,), 0, ROWS_DEV)
        return picked * ROWS_DEV + local_row
    stored = jax.vmap(one_block)(block_keys).reshape(USERS, LENGTH)
    return (storage, inverse[stored].astype(jnp.int32))


def draw_row_place(key, part):
    storage, identities = make_rows(key)
    return storage


def draw_item_ids(key, part):
    storage, identities = make_rows(key)
    return identities


def draw_history_len(key, part):
    lengths = jax.random.randint(jax.random.fold_in(key, 21), (USERS,), LENGTH // 4, LENGTH + 1)
    full_user = jax.random.randint(jax.random.fold_in(key, 22), (), 0, USERS)
    return jnp.where(jnp.arange(USERS) == full_user, LENGTH, lengths).astype(jnp.int32)


def draw_out_cotangent(key, part):
    own_key = jax.random.fold_in(key, 31)
    place = jnp.arange(LENGTH, dtype=jnp.float32) / (LENGTH - 1)
    ramp = 0.1 * jnp.exp(jnp.log(30.0) * place)
    base = jnp.clip(jax.random.normal(own_key, (USERS, LENGTH, D), jnp.float32), -6.0, 6.0)
    return (base * ramp[None, :, None]).astype(jnp.bfloat16)


def steps_of(rng, dims, cuts, least, top_value):
    def one(dim, blocks):
        heights = jax.random.uniform(jax.random.fold_in(jax.random.fold_in(rng, 6), dim), (blocks,), jnp.float32, least / len(cuts), top_value / len(cuts))
        return jnp.repeat(jnp.exp(heights), dims[dim] // blocks).reshape((-1,) + (1,) * (len(dims) - dim - 1))

    loudness = one(*cuts[0])
    for cut in cuts[1:]:
        loudness = loudness * one(*cut)
    return loudness


def bell_draw(key, shape, width, most, cuts=(), kind=jnp.bfloat16):
    entries = width * jax.random.normal(key, shape, jnp.float32)
    if cuts:
        entries = entries * steps_of(key, shape, cuts, -0.22, 0.18)
    return jnp.clip(entries, -most, most).astype(kind)


def setup_inputs(seed: int = 0) -> dict:
    key_of = jax.random.split(jax.random.key(seed), 8)
    item_ids = draw_item_ids(jax.random.fold_in(key_of[7], 71), 0)
    history_len = draw_history_len(jax.random.fold_in(key_of[7], 71), 0)
    row_place = draw_row_place(jax.random.fold_in(key_of[7], 71), 0)
    item_table = bell_draw(key_of[3], (VOCAB, D), 1.0, 6.0, ((0, 128),))
    input_proj = bell_draw(key_of[4], (D, 4 * D), D ** -0.5, 0.25)
    output_proj = bell_draw(key_of[5], (D, D), D ** -0.5, 0.25)
    out_cotangent = draw_out_cotangent(jax.random.fold_in(key_of[7], 71), 0)
    return dict(item_ids=item_ids, history_len=history_len, row_place=row_place, item_table=item_table, input_proj=input_proj, output_proj=output_proj, out_cotangent=out_cotangent)


eps_norm = 1e-05

def dsilu(inputs):
    sigmoid_part = jax.nn.sigmoid(inputs)
    return sigmoid_part * (1.0 + inputs * (1.0 - sigmoid_part))

def normalize(inputs):
    centred = inputs - lax.optimization_barrier(jnp.mean(inputs, axis=-1, keepdims=True))
    spread = jnp.sqrt(lax.optimization_barrier(jnp.mean(centred * centred, axis=-1, keepdims=True)) + eps_norm)
    return (centred / spread, spread)

def norm_back(gradient, normed, spread):
    mean_grad = lax.optimization_barrier(jnp.mean(gradient, axis=-1, keepdims=True))
    mean_prod = lax.optimization_barrier(jnp.mean(gradient * normed, axis=-1, keepdims=True))
    return (gradient - mean_grad - normed * mean_prod) / spread

def heads_view(matrix):
    return matrix.astype(jnp.float32).reshape(matrix.shape[0], HEADS, HEAD_DIM)

def tile_mask(query_pos, key_pos, length_user):
    return (key_pos[None, :] <= query_pos[:, None]) & (query_pos[:, None] < length_user)

def tile_forward(queries, keys_blk, values_blk, allowed, score_scale):
    scores = jnp.einsum('lhe,nhe->hln', heads_view(queries), heads_view(keys_blk)) * score_scale
    weights = jnp.where(allowed[None], jax.nn.silu(scores), 0.0).astype(jnp.bfloat16)
    result = jnp.einsum('hln,nhe->lhe', weights.astype(jnp.float32), heads_view(values_blk))
    return result.reshape(queries.shape[0], -1)

def tile_query_grad(queries, grad_rows, keys_blk, values_blk, allowed, score_scale):
    scores = jnp.einsum('lhe,nhe->hln', heads_view(queries), heads_view(keys_blk)) * score_scale
    weight_grad = jnp.einsum('lhe,nhe->hln', heads_view(grad_rows), heads_view(values_blk))
    score_grad = jnp.where(allowed[None], weight_grad * dsilu(scores), 0.0).astype(jnp.bfloat16)
    result = jnp.einsum('hln,nhe->lhe', score_grad.astype(jnp.float32), heads_view(keys_blk))
    return result.reshape(queries.shape[0], -1) * score_scale

def tile_key_grad(query_piece, grad_piece, keys_mine, values_mine, allowed, score_scale):
    scores = jnp.einsum('lhe,nhe->hln', heads_view(query_piece), heads_view(keys_mine)) * score_scale
    weights = jnp.where(allowed[None], jax.nn.silu(scores), 0.0).astype(jnp.bfloat16)
    weight_grad = jnp.einsum('lhe,nhe->hln', heads_view(grad_piece), heads_view(values_mine))
    score_grad = jnp.where(allowed[None], weight_grad * dsilu(scores), 0.0).astype(jnp.bfloat16)
    value_part = jnp.einsum('hln,lhe->nhe', weights.astype(jnp.float32), heads_view(grad_piece))
    key_part = jnp.einsum('hln,lhe->nhe', score_grad.astype(jnp.float32), heads_view(query_piece))
    key_count = keys_mine.shape[0]
    return (key_part.reshape(key_count, -1) * score_scale, value_part.reshape(key_count, -1))

def block_sweep(tile_fn, outer, inner, starts, zeros_out, needed):

    def per_outer(outer_item):
        outer_blocks, outer_start = outer_item

        def per_inner(running, inner_item):
            inner_blocks, inner_start = inner_item

            def work():
                return tile_fn(running, outer_blocks, inner_blocks, outer_start, inner_start)
            return (lax.cond(needed(outer_start, inner_start), work, lambda: running), None)
        result, unused = lax.scan(per_inner, zeros_out, (inner, starts))
        return result
    return lax.map(per_outer, (outer, starts))

def one_user(user_item, item_table, input_proj, output_proj, score_scale):
    stored_user, length_user, cot_user = user_item
    block_rows = math.gcd(LENGTH, 512)
    block_count = LENGTH // block_rows
    local_pos = jnp.arange(block_rows, dtype=jnp.int32)
    starts = jnp.arange(block_count, dtype=jnp.int32) * block_rows
    positions = jnp.arange(LENGTH, dtype=jnp.int32)
    live_rows = (positions < length_user).astype(jnp.float32)[:, None]
    embedded = item_table[stored_user]
    normed_exact, input_spread = normalize(embedded.astype(jnp.float32))
    normed = normed_exact.astype(jnp.bfloat16)
    pre_act = jnp.dot(normed, input_proj, preferred_element_type=jnp.float32)
    activated = jax.nn.silu(pre_act)
    gate_u = activated[:, :D]
    value_rows = activated[:, D:2 * D].astype(jnp.bfloat16)
    query_rows = activated[:, 2 * D:3 * D].astype(jnp.bfloat16)
    key_rows = activated[:, 3 * D:].astype(jnp.bfloat16)

    def blocks(matrix):
        return matrix.reshape(block_count, block_rows, matrix.shape[1])
    zero_rows = jnp.zeros((block_rows, D), jnp.float32)

    def query_needed(query_start, key_start):
        return (key_start <= query_start + block_rows - 1) & (query_start < length_user)

    def key_needed(key_start, query_start):
        return (query_start + block_rows - 1 >= key_start) & (query_start < length_user) & (key_start < length_user)

    def forward_tile(running, outer_blocks, inner_blocks, query_start, key_start):
        allowed = tile_mask(query_start + local_pos, key_start + local_pos, length_user)
        return running + tile_forward(outer_blocks[0], inner_blocks[0], inner_blocks[1], allowed, score_scale)
    attention = block_sweep(forward_tile, (blocks(query_rows),), (blocks(key_rows), blocks(value_rows)), starts, zero_rows, query_needed).reshape(LENGTH, D)
    attn_normed, attn_spread = normalize(attention)
    mixed = (attn_normed * gate_u).astype(jnp.bfloat16)
    branch = jnp.dot(mixed, output_proj, preferred_element_type=jnp.float32)
    layer_out = (live_rows * (embedded.astype(jnp.float32) + branch)).astype(jnp.bfloat16)
    cot_masked = jnp.where(live_rows > 0.0, cot_user, 0.0).astype(jnp.bfloat16)
    mixed_grad = jnp.dot(cot_masked, output_proj.T, preferred_element_type=jnp.float32)
    attention_grad = norm_back(mixed_grad * gate_u, attn_normed, attn_spread).astype(jnp.bfloat16)

    def query_tile(running, outer_blocks, inner_blocks, query_start, key_start):
        allowed = tile_mask(query_start + local_pos, key_start + local_pos, length_user)
        return running + tile_query_grad(outer_blocks[0], outer_blocks[1], inner_blocks[0], inner_blocks[1], allowed, score_scale)
    query_grad = block_sweep(query_tile, (blocks(query_rows), blocks(attention_grad)), (blocks(key_rows), blocks(value_rows)), starts, zero_rows, query_needed).reshape(LENGTH, D)

    def key_tile(running, outer_blocks, inner_blocks, key_start, query_start):
        allowed = tile_mask(query_start + local_pos, key_start + local_pos, length_user)
        key_part, value_part = tile_key_grad(inner_blocks[0], inner_blocks[1], outer_blocks[0], outer_blocks[1], allowed, score_scale)
        return (running[0] + key_part, running[1] + value_part)
    key_grad, value_grad = block_sweep(key_tile, (blocks(key_rows), blocks(value_rows)), (blocks(query_rows), blocks(attention_grad)), starts, (zero_rows, zero_rows), key_needed)
    key_grad = key_grad.reshape(LENGTH, D)
    value_grad = value_grad.reshape(LENGTH, D)
    activated_grad = jnp.concatenate([mixed_grad * attn_normed, value_grad, query_grad, key_grad], axis=1)
    pre_grad = (activated_grad * dsilu(pre_act)).astype(jnp.bfloat16)
    norm_grad = jnp.dot(pre_grad, input_proj.T, preferred_element_type=jnp.float32)
    embed_grad = cot_masked.astype(jnp.float32) + norm_back(norm_grad, normed_exact, input_spread)
    return (layer_out, embed_grad)

def reference(item_ids, history_len, row_place, item_table, input_proj, output_proj, out_cotangent):
    score_scale = HEAD_DIM ** (-0.5)
    stored_rows = row_place[item_ids].astype(jnp.int32)

    def per_user(user_item):
        return one_user(user_item, item_table, input_proj, output_proj, score_scale)
    layer_out, embed_grad = lax.map(per_user, (stored_rows, history_len, out_cotangent))
    table_sum = jnp.zeros((VOCAB, D), jnp.float32).at[stored_rows.reshape(-1)].add(embed_grad.reshape(-1, D))
    return (layer_out, table_sum.astype(jnp.bfloat16))
```

```python
import functools

import jax
import jax.numpy as jnp
from jax import lax
from jax.experimental import pallas as pl
from jax.experimental.pallas import tpu as pltpu
from jax.sharding import PartitionSpec as P

HEADS = 8
CAP = 6
EPS = 1e-05
F32 = jnp.float32
BF = jnp.bfloat16
MESH = pl.DeviceIdType.MESH
VM = pl.BlockSpec(memory_space=pltpu.VMEM)
SM = pl.BlockSpec(memory_space=pltpu.SMEM)
TABLE, SEQ = 8, 16
OWNERS = TABLE * SEQ
LEN = 256
HD = 64
WIDTH = 512
PIECES = CAP * WIDTH // 128
CHUNK = 2 * LEN
CHUNKS = SEQ // 2
VMEM_LIMIT = 56 * 2**20


def nn(a, b):
    return lax.dot_general(a, b, (((1,), (0,)), ((), ())), preferred_element_type=F32)


def nt(a, b):
    return lax.dot_general(a, b, (((1,), (1,)), ((), ())), preferred_element_type=F32)


def iota(shape, dim):
    return lax.broadcasted_iota(jnp.int32, shape, dim)


def silu(x):
    u = 0.5 * x
    return u + u * jnp.tanh(u)


def dsilu(x):
    u = 0.5 * x
    th = jnp.tanh(u)
    return (0.5 + 0.5 * th) * (1.0 + u * (1.0 - th))


def mean_last(x):
    return jnp.mean(x, axis=-1, keepdims=True)


def normalize(x):
    centred = x - mean_last(x)
    spread = jnp.sqrt(mean_last(centred * centred) + EPS)
    return centred / spread, spread


def norm_back(gradient, normed, spread):
    return (gradient - mean_last(gradient) - normed * mean_last(gradient * normed)) / spread


def places():
    t = lax.axis_index("table")
    s = lax.axis_index("seq")
    return t, s


def barrier_all():
    t, s = places()
    me = t * SEQ + s
    sem = pltpu.get_barrier_semaphore()

    def body(i, carry):
        d = lax.rem(me + i, OWNERS)
        pl.semaphore_signal(
            sem, inc=1, device_id=(d // SEQ, lax.rem(d, SEQ)), device_id_type=MESH
        )
        return carry

    lax.fori_loop(1, OWNERS, body, 0)
    pl.semaphore_wait(sem, OWNERS - 1)


def barrier_plane():
    t, s = places()
    base = t // 2 * 2
    me = lax.rem(t, 2) * SEQ + s
    sem = pltpu.get_barrier_semaphore()

    def body(i, carry):
        d = lax.rem(me + i, 2 * SEQ)
        pl.semaphore_signal(
            sem, inc=1, device_id=(base + d // SEQ, lax.rem(d, SEQ)), device_id_type=MESH
        )
        return carry

    lax.fori_loop(1, 2 * SEQ, body, 0)
    pl.semaphore_wait(sem, 2 * SEQ - 1)


def remote(src, dst, send_sem, recv_sem, t, s):
    return pltpu.make_async_remote_copy(
        src_ref=src,
        dst_ref=dst,
        send_sem=send_sem,
        recv_sem=recv_sem,
        device_id=(t, s),
        device_id_type=MESH,
    )


def wait_bytes(ref, sem):
    pltpu.make_async_copy(ref, ref, sem).wait()


def all_to_all(out_ref, in_ref, send_sem, recv_sem, group_ready):
    t, s = places()
    me = t * SEQ + s

    def group(g, carry):
        tt = lax.rem(t + g, TABLE)
        group_ready(tt)

        def one(i, carry2):
            ss = lax.rem(s + i, SEQ)
            d = tt * SEQ + ss

            @pl.when(d != me)
            def _():
                remote(out_ref.at[d], in_ref.at[me], send_sem, recv_sem, tt, ss).start()

            return carry2

        lax.fori_loop(0, SEQ, one, 0)
        return carry

    lax.fori_loop(0, TABLE, group, 0)
    in_ref[me] = out_ref[me]


def all_to_all_wait(out_ref, in_ref, send_sem, recv_sem):
    wait_bytes(in_ref.at[pl.ds(0, OWNERS - 1)], recv_sem)
    wait_bytes(out_ref.at[pl.ds(0, OWNERS - 1)], send_sem)


def rows_kernel(
    ids_ref, table_ref, ans_ref, want_ref, all_ids, ids2d, acc, spread_buf, outbuf, sems
):
    t, s = places()
    me = t * SEQ + s
    rows_dev = table_ref.shape[0]
    all_ids[me] = ids_ref[...]
    barrier_all()

    def plane(i, carry):
        ss = lax.rem(s + i, SEQ)
        remote(all_ids.at[me], all_ids.at[me], sems.at[0], sems.at[1], t, ss).start()
        return carry

    lax.fori_loop(1, SEQ, plane, 0)
    wait_bytes(all_ids.at[pl.ds(0, SEQ - 1)], sems.at[1])
    mine = all_ids.at[pl.ds(t * SEQ, SEQ)]

    def column(i, carry):
        tt = lax.rem(t + i, TABLE)
        remote(mine, mine, sems.at[2], sems.at[3], tt, s).start()
        return carry

    lax.fori_loop(1, TABLE, column, 0)
    wait_bytes(all_ids.at[pl.ds(0, (TABLE - 1) * SEQ)], sems.at[3])

    def flat(b, carry):
        ids2d[pl.ds(b, 1), :] = all_ids[b]
        return carry

    lax.fori_loop(0, OWNERS, flat, 0, unroll=8)
    ids = ids2d[...]
    hit = ids // rows_dev == me
    local_row = lax.rem(ids, rows_dev).astype(F32)
    before = (iota((LEN, LEN), 0) < iota((LEN, LEN), 1)).astype(BF)
    rank = nn(hit.astype(BF), before)
    value = jnp.where(hit, local_row + 1.0, 0.0)
    wanted = []
    for r in range(CAP):
        got = jnp.sum(jnp.where(rank == r, value, 0.0), axis=1, keepdims=True) - 1.0
        wanted.append(got.astype(jnp.int32))
    lane = iota((OWNERS, OWNERS), 1)
    square = jnp.full((OWNERS, OWNERS), -1.0, F32)
    for r in range(CAP):
        square = jnp.where(lane == r, wanted[r].astype(F32), square)
    want_ref[...] = square.T[:8].astype(jnp.int32)

    block = 512

    def gather(j, carry):
        base = j * block
        table_blk = table_ref[pl.ds(pl.multiple_of(base, block), block), :]
        cols = iota((OWNERS, block), 1) + base
        pick = jnp.concatenate([(w == cols).astype(F32).astype(BF) for w in wanted], axis=0)
        part = nn(pick, table_blk)

        @pl.when(j == 0)
        def _():
            acc[...] = part

        @pl.when(j > 0)
        def _():
            acc[...] += part

        return carry

    lax.fori_loop(0, rows_dev // block, gather, 0)
    for r in range(CAP):
        for q in range(WIDTH // 128):
            spread_buf[pl.ds(r * 4 + q, OWNERS, stride=PIECES), :] = acc[
                r * OWNERS : (r + 1) * OWNERS, q * 128 : (q + 1) * 128
            ]

    def group_ready(tt):
        rows = SEQ * PIECES
        chunk = spread_buf[pl.ds(pl.multiple_of(tt * rows, rows), rows), :]
        outbuf[pl.ds(tt * SEQ, SEQ)] = chunk.astype(BF).reshape(SEQ, PIECES, 128)

    all_to_all(outbuf, ans_ref, sems.at[4], sems.at[5], group_ready)
    wait_bytes(all_ids.at[pl.ds(0, SEQ - 1)], sems.at[0])
    wait_bytes(all_ids.at[pl.ds(0, (TABLE - 1) * SEQ)], sems.at[2])
    all_to_all_wait(outbuf, ans_ref, sems.at[4], sems.at[5])


def fetch_rows(stored_row, item_table):
    return pl.pallas_call(
        rows_kernel,
        out_shape=(
            jax.ShapeDtypeStruct((OWNERS, PIECES, 128), BF),
            jax.ShapeDtypeStruct((8, OWNERS), jnp.int32),
        ),
        in_specs=[VM, VM],
        out_specs=(VM, VM),
        scratch_shapes=[
            pltpu.VMEM((OWNERS, 1, LEN), jnp.int32),
            pltpu.VMEM((OWNERS, LEN), jnp.int32),
            pltpu.VMEM((CAP * OWNERS, WIDTH), F32),
            pltpu.VMEM((OWNERS * PIECES, 128), F32),
            pltpu.VMEM((OWNERS, PIECES, 128), BF),
            pltpu.SemaphoreType.DMA((6,)),
        ],
        compiler_params=pltpu.CompilerParams(
            collective_id=0, has_side_effects=True, vmem_limit_bytes=VMEM_LIMIT
        ),
        name="rows",
    )(stored_row, item_table)


def unpack_rows(packed_ref, spread_buf, rows_buf):
    spread_buf[...] = packed_ref[...].astype(F32).reshape(OWNERS * PIECES, 128)
    for r in range(CAP):
        for q in range(WIDTH // 128):
            rows_buf[r * OWNERS : (r + 1) * OWNERS, q * 128 : (q + 1) * 128] = spread_buf[
                pl.ds(r * 4 + q, OWNERS, stride=PIECES), :
            ].astype(BF)


def query_block(core, k):
    return 2 * k + lax.rem(k + core, 2)


def query_core(s):
    return lax.rem((s + 1) // 2, 2)


def layer_kernel(
    stored_ref, len_ref, ans_ref, win_ref, wo_ref, cot_ref,
    out_ref, grads_ref,
    spread_buf, rows_buf, emb, norm_exact, in_spread, pre, gate, mixed_grad,
    qkv_send, qkv_all, key_nat, value_nat, key_t, value_t,
    o_send, o_all, attn_norm, d_send, d_all,
    dkv_acc, dkv_peer, dkv_send, dkv_all, dq_send, dq_all, qd_pad,
    sem, qkv_sem, relay_sem, d_sem, peer_sem,
):
    t, s = places()
    core = lax.rem(t, 2)
    plane = t - core
    head_user = s // HEADS
    head = lax.rem(s, HEADS)
    owner_t = plane + head_user
    my_user = core
    my_core = query_core(s)
    my_slot = s // 2

    def send(src, dst, send_sem, recv_sem, tt, ss):
        local = (tt == t) & (ss == s)

        @pl.when(local)
        def _():
            pltpu.make_async_copy(src, dst, recv_sem).start()

        @pl.when(jnp.logical_not(local))
        def _():
            remote(src, dst, send_sem, recv_sem, tt, ss).start()

    def sent(src, send_sem, tt, ss):
        @pl.when(jnp.logical_not((tt == t) & (ss == s)))
        def _():
            wait_bytes(src, send_sem)

    unpack_rows(ans_ref, spread_buf, rows_buf)
    stored = stored_ref[...]
    owner = stored // 4096
    owned = (iota((LEN, OWNERS), 1) == owner).astype(F32)
    earlier = (iota((LEN, LEN), 1) < iota((LEN, LEN), 0)).astype(BF)
    rank = jnp.sum(nn(earlier, owned.astype(BF)) * owned, axis=1, keepdims=True)
    slot = rank.astype(jnp.int32) * OWNERS + owner
    pick = (iota((LEN, CAP * OWNERS), 1) == slot).astype(F32).astype(BF)
    embedded = nn(pick, rows_buf[...])
    emb[...] = embedded
    normed, spread = normalize(embedded)
    norm_exact[...] = normed
    in_spread[...] = jnp.broadcast_to(spread, (LEN, 128))
    pre[...] = nn(normed.astype(BF), win_ref[...])
    for g in range(HEADS // 2):
        for part, (first, scale) in enumerate(((2, 0.0625), (3, 1.0), (1, 1.0))):
            low = first * WIDTH + g * 128
            act = silu(pre[:, low : low + 128]).astype(BF).astype(F32) * scale
            turned = act.T.astype(BF)
            qkv_send[2 * g, part * HD : (part + 1) * HD, :] = turned[:HD]
            qkv_send[2 * g + 1, part * HD : (part + 1) * HD, :] = turned[HD:]

    barrier_plane()

    def send_qkv(i, carry):
        h = lax.rem(i + s, HEADS)
        send(
            qkv_send.at[h], qkv_all.at[s], sem.at[0], qkv_sem.at[my_slot],
            plane + my_core, my_user * HEADS + h,
        )
        return carry

    lax.fori_loop(0, HEADS, send_qkv, 0)

    positions = s * LEN + iota((LEN, 1), 0)
    live = positions < len_ref[0]
    cot = jnp.where(live, cot_ref[...].astype(F32), 0.0)
    mixed_grad[...] = nt(cot.astype(BF), wo_ref[...])
    gate[...] = silu(pre[:, :WIDTH])

    peer = plane + 1 - core

    def relay(k):
        i = query_block(core, k)
        wait_bytes(qkv_all.at[i], qkv_sem.at[k])
        ref = qkv_all.at[i, pl.ds(HD, 2 * HD)]
        remote(ref, ref, sem.at[1], relay_sem.at[k], peer, s).start()

    relay(0)

    def forward(k, carry):
        @pl.when(k < CHUNKS - 1)
        def _():
            relay(k + 1)

        wait_bytes(qkv_all.at[0, pl.ds(HD, 2 * HD)], relay_sem.at[k])
        for half in range(2):
            both = qkv_all[2 * k + half]
            rows = slice(half * LEN, (half + 1) * LEN)
            key_t[k, :, rows] = both[HD : 2 * HD]
            value_t[k, :, rows] = both[2 * HD :]
            key_nat[k, rows, :] = both[HD : 2 * HD].T
            value_nat[k, rows, :] = both[2 * HD :].T
        query = qkv_all[query_block(core, k), :HD]

        def tile(j, allowed):
            u = nn(key_nat[j], query)
            if allowed is not None:
                u = jnp.where(allowed, u, 0.0)
            return nn(value_t[j], (u + u * jnp.tanh(u)).astype(BF))

        total = lax.fori_loop(
            0, k, lambda j, o: o + tile(j, None), jnp.zeros((HD, LEN), F32)
        )
        offset = lax.rem(k + core, 2) * LEN
        allowed = iota((CHUNK, LEN), 0) <= iota((CHUNK, LEN), 1) + offset
        o_send[k] = (total + tile(k, allowed)).astype(BF)
        send(
            o_send.at[k], o_all.at[head], sem.at[2], sem.at[3],
            owner_t, query_block(core, k),
        )
        return carry

    lax.fori_loop(0, CHUNKS, forward, 0)

    wait_bytes(o_all, sem.at[3])
    attention = o_all[...].reshape(WIDTH, LEN).astype(F32).T
    attention = jnp.where(live, attention, 0.0)
    attn, attn_spread = normalize(attention)
    attn_norm[...] = attn
    dz = mixed_grad[...] * gate[...]
    attention_grad = norm_back(dz, attn, attn_spread).astype(BF).astype(F32)
    d_send[...] = (0.5 * attention_grad).T.astype(BF).reshape(HEADS, HD, LEN)

    def send_d(i, carry):
        h = lax.rem(i + s, HEADS)
        send(
            d_send.at[h], d_all.at[my_slot], sem.at[4], d_sem.at[my_slot],
            plane + my_core, my_user * HEADS + h,
        )
        return carry

    lax.fori_loop(0, HEADS, send_d, 0)
    mixed = (attn * gate[...]).astype(BF)
    branch = nn(mixed, wo_ref[...])
    out_ref[...] = jnp.where(live, emb[...] + branch, 0.0).astype(BF)

    dkv_acc[...] = jnp.zeros_like(dkv_acc)
    qd_pad[...] = jnp.zeros_like(qd_pad)

    def reduce_keys(k):
        wait_bytes(dkv_peer.at[k], peer_sem.at[k])
        half = lax.rem(k + core, 2)
        own = dkv_acc[k, pl.ds(pl.multiple_of(half * LEN, LEN), LEN), :]
        dkv_send[k] = (2.0 * (own + dkv_peer[k])).astype(BF)
        send(
            dkv_send.at[k], dkv_all.at[head], sem.at[5], sem.at[6],
            owner_t, query_block(core, k),
        )

    def peer_half(k):
        half = 1 - lax.rem(k + core, 2)
        return dkv_acc.at[k, pl.ds(pl.multiple_of(half * LEN, LEN), LEN)]

    def backward(step, carry):
        k = CHUNKS - 1 - step
        wait_bytes(d_all.at[k], d_sem.at[k])
        query = qkv_all[query_block(core, k), :HD]
        grad = d_all[k]
        qd_pad[:LEN, :HD] = query.T
        qd_pad[LEN:, HD:] = grad.T
        pair = qd_pad[...]

        def tile(j, allowed):
            u = nn(key_nat[j], query)
            dp = nn(value_nat[j], grad)
            th = jnp.tanh(u)
            a = 1.0 + th
            p = u * a
            ds = dp * (a * (1.0 + u * (1.0 - th)))
            if allowed is not None:
                p = jnp.where(allowed, p, 0.0)
                ds = jnp.where(allowed, ds, 0.0)
            p = p.astype(BF)
            ds = ds.astype(BF)
            dkv_acc[j] += nn(ds, pair[:LEN]) + nn(p, pair[LEN:])
            return nn(key_t[j], ds)

        total = lax.fori_loop(
            0, k, lambda j, o: o + tile(j, None), jnp.zeros((HD, LEN), F32)
        )
        offset = lax.rem(k + core, 2) * LEN
        allowed = iota((CHUNK, LEN), 0) <= iota((CHUNK, LEN), 1) + offset
        dq_send[k] = (0.125 * (total + tile(k, allowed))).astype(BF)
        send(
            dq_send.at[k], dq_all.at[head], sem.at[7], sem.at[8],
            owner_t, query_block(core, k),
        )
        remote(peer_half(k), dkv_peer.at[k], sem.at[9], peer_sem.at[k], peer, s).start()

        @pl.when(step > 0)
        def _():
            reduce_keys(k + 1)

        return carry

    lax.fori_loop(0, CHUNKS, backward, 0)
    reduce_keys(0)

    wait_bytes(dq_all, sem.at[8])
    wait_bytes(dkv_all, sem.at[6])

    def pre_grad(first, gradient):
        return (gradient * dsilu(pre[:, first * WIDTH : (first + 1) * WIDTH])).astype(BF)

    def by_head(low):
        return jnp.concatenate(
            [dkv_all[h][:, low : low + HD].astype(F32) for h in range(HEADS)], axis=1
        )

    def back(first, gradient):
        return nt(pre_grad(first, gradient), win_ref[:, first * WIDTH : (first + 1) * WIDTH])

    norm_grad = back(0, mixed_grad[...] * attn_norm[...])
    norm_grad += back(1, by_head(HD))
    norm_grad += back(2, dq_all[...].reshape(WIDTH, LEN).astype(F32).T)
    norm_grad += back(3, by_head(0))
    cot = jnp.where(live, cot_ref[...].astype(F32), 0.0)
    embed_grad = cot + norm_back(norm_grad, norm_exact[...], in_spread[:, :1])
    put = lax.dot_general(
        pick, embed_grad.astype(BF), (((0,), (0,)), ((), ())), preferred_element_type=F32
    )
    for r in range(CAP):
        for q in range(WIDTH // 128):
            spread_buf[pl.ds(r * 4 + q, OWNERS, stride=PIECES), :] = put[
                r * OWNERS : (r + 1) * OWNERS, q * 128 : (q + 1) * 128
            ]
    grads_ref[...] = spread_buf[...].astype(BF).reshape(OWNERS, PIECES, 128)

    def drain(i, carry):
        sent(qkv_send.at[0], sem.at[0], plane + my_core, my_user * HEADS + i)
        sent(d_send.at[0], sem.at[4], plane + my_core, my_user * HEADS + i)
        wait_bytes(qkv_all.at[0, pl.ds(HD, 2 * HD)], sem.at[1])
        wait_bytes(dkv_peer.at[0], sem.at[9])
        block = query_block(core, i)
        sent(o_send.at[0], sem.at[2], owner_t, block)
        sent(dkv_send.at[0], sem.at[5], owner_t, block)
        sent(dq_send.at[0], sem.at[7], owner_t, block)
        return carry

    lax.fori_loop(0, CHUNKS, drain, 0)


def layer(stored_col, length, answers, input_proj, output_proj, cot):
    return pl.pallas_call(
        layer_kernel,
        out_shape=(
            jax.ShapeDtypeStruct((LEN, WIDTH), BF),
            jax.ShapeDtypeStruct((OWNERS, PIECES, 128), BF),
        ),
        in_specs=[VM, SM, VM, VM, VM, VM],
        out_specs=(VM, VM),
        scratch_shapes=[
            pltpu.VMEM((OWNERS * PIECES, 128), F32),
            pltpu.VMEM((CAP * OWNERS, WIDTH), BF),
            pltpu.VMEM((LEN, WIDTH), F32),
            pltpu.VMEM((LEN, WIDTH), F32),
            pltpu.VMEM((LEN, 128), F32),
            pltpu.VMEM((LEN, 4 * WIDTH), F32),
            pltpu.VMEM((LEN, WIDTH), F32),
            pltpu.VMEM((LEN, WIDTH), F32),
            pltpu.VMEM((HEADS, 3 * HD, LEN), BF),
            pltpu.VMEM((SEQ, 3 * HD, LEN), BF),
            pltpu.VMEM((CHUNKS, CHUNK, HD), BF),
            pltpu.VMEM((CHUNKS, CHUNK, HD), BF),
            pltpu.VMEM((CHUNKS, HD, CHUNK), BF),
            pltpu.VMEM((CHUNKS, HD, CHUNK), BF),
            pltpu.VMEM((CHUNKS, HD, LEN), BF),
            pltpu.VMEM((HEADS, HD, LEN), BF),
            pltpu.VMEM((LEN, WIDTH), F32),
            pltpu.VMEM((HEADS, HD, LEN), BF),
            pltpu.VMEM((CHUNKS, HD, LEN), BF),
            pltpu.VMEM((CHUNKS, CHUNK, 2 * HD), F32),
            pltpu.VMEM((CHUNKS, LEN, 2 * HD), F32),
            pltpu.VMEM((CHUNKS, LEN, 2 * HD), BF),
            pltpu.VMEM((HEADS, LEN, 2 * HD), BF),
            pltpu.VMEM((CHUNKS, HD, LEN), BF),
            pltpu.VMEM((HEADS, HD, LEN), BF),
            pltpu.VMEM((2 * LEN, 2 * HD), BF),
            pltpu.SemaphoreType.DMA((10,)),
            pltpu.SemaphoreType.DMA((CHUNKS,)),
            pltpu.SemaphoreType.DMA((CHUNKS,)),
            pltpu.SemaphoreType.DMA((CHUNKS,)),
            pltpu.SemaphoreType.DMA((CHUNKS,)),
        ],
        compiler_params=pltpu.CompilerParams(
            collective_id=1, has_side_effects=True, vmem_limit_bytes=VMEM_LIMIT
        ),
        name="layer",
    )(stored_col, length, answers, input_proj, output_proj, cot)


def grads_kernel(out_ref, in_ref, sems):
    barrier_all()
    all_to_all(out_ref, in_ref, sems.at[0], sems.at[1], lambda tt: None)
    all_to_all_wait(out_ref, in_ref, sems.at[0], sems.at[1])


def exchange_grads(outgoing):
    return pl.pallas_call(
        grads_kernel,
        out_shape=jax.ShapeDtypeStruct(outgoing.shape, outgoing.dtype),
        in_specs=[VM],
        out_specs=VM,
        scratch_shapes=[pltpu.SemaphoreType.DMA((2,))],
        compiler_params=pltpu.CompilerParams(
            collective_id=2, has_side_effects=True, vmem_limit_bytes=VMEM_LIMIT
        ),
        name="grads",
    )(outgoing)


def sum_kernel(block, want_ref, packed_ref, out_ref, spread_buf, rows_buf):
    j = pl.program_id(0)

    @pl.when(j == 0)
    def _():
        unpack_rows(packed_ref, spread_buf, rows_buf)

    rows = iota((block, OWNERS), 0) + j * block
    pick = jnp.concatenate(
        [(want_ref[r : r + 1, :] == rows).astype(F32).astype(BF) for r in range(CAP)], axis=1
    )
    out_ref[...] = nn(pick, rows_buf[...]).astype(BF)


def sum_rows(wanted, arrived, rows_dev):
    block = 512
    return pl.pallas_call(
        functools.partial(sum_kernel, block),
        out_shape=jax.ShapeDtypeStruct((rows_dev, WIDTH), BF),
        grid=(rows_dev // block,),
        in_specs=[
            pl.BlockSpec((8, OWNERS), lambda j: (0, 0)),
            pl.BlockSpec((OWNERS, PIECES, 128), lambda j: (0, 0, 0)),
        ],
        out_specs=pl.BlockSpec((block, WIDTH), lambda j: (j, 0)),
        scratch_shapes=[
            pltpu.VMEM((OWNERS * PIECES, 128), F32),
            pltpu.VMEM((CAP * OWNERS, WIDTH), BF),
        ],
        compiler_params=pltpu.CompilerParams(vmem_limit_bytes=VMEM_LIMIT),
        name="sums",
    )(wanted, arrived)


def local(item_ids, history_len, row_place, item_table, input_proj, output_proj, out_cotangent):
    stored = row_place[item_ids[0]]
    answers, wanted = fetch_rows(stored[None, :], item_table)
    layer_out, outgoing = layer(
        stored[:, None], history_len, answers, input_proj, output_proj, out_cotangent[0]
    )
    arrived = exchange_grads(outgoing)
    table_grad = sum_rows(wanted, arrived, item_table.shape[0])
    return layer_out[None], table_grad


def solution(mesh):
    placed = (
        P("table", "seq"),
        P("table"),
        P(),
        P(("table", "seq"), None),
        P(),
        P(),
        P("table", "seq", None),
    )
    return jax.shard_map(
        local,
        mesh=mesh,
        in_specs=placed,
        out_specs=(P("table", "seq", None), P(("table", "seq"), None)),
        check_vma=False,
    )
```

```python
import functools

import jax
import jax.numpy as jnp
from jax import lax
from jax.experimental import pallas as pl
from jax.experimental.pallas import tpu as pltpu
from jax.sharding import PartitionSpec as P

HEADS = 8
CAP = 6
EPS = 1e-05
F32 = jnp.float32
BF = jnp.bfloat16
MESH = pl.DeviceIdType.MESH
VM = pl.BlockSpec(memory_space=pltpu.VMEM)
SM = pl.BlockSpec(memory_space=pltpu.SMEM)
TABLE, SEQ = 8, 16
OWNERS = TABLE * SEQ
LEN = 256
HD = 64
WIDTH = 512
PIECES = CAP * WIDTH // 128
CHUNK = 2 * LEN
CHUNKS = SEQ // 2
VMEM_LIMIT = 56 * 2**20


def nn(a, b):
    return lax.dot_general(a, b, (((1,), (0,)), ((), ())), preferred_element_type=F32)


def nt(a, b):
    return lax.dot_general(a, b, (((1,), (1,)), ((), ())), preferred_element_type=F32)


def iota(shape, dim):
    return lax.broadcasted_iota(jnp.int32, shape, dim)


def silu(x):
    u = 0.5 * x
    return u + u * jnp.tanh(u)


def dsilu(x):
    u = 0.5 * x
    th = jnp.tanh(u)
    return (0.5 + 0.5 * th) * (1.0 + u * (1.0 - th))


def mean_last(x):
    return jnp.mean(x, axis=-1, keepdims=True)


def normalize(x):
    centred = x - mean_last(x)
    spread = jnp.sqrt(mean_last(centred * centred) + EPS)
    return centred / spread, spread


def norm_back(gradient, normed, spread):
    return (gradient - mean_last(gradient) - normed * mean_last(gradient * normed)) / spread


def places():
    t = lax.axis_index("table")
    s = lax.axis_index("seq")
    return t, s


def barrier_all():
    t, s = places()
    me = t * SEQ + s
    sem = pltpu.get_barrier_semaphore()

    def body(i, carry):
        d = lax.rem(me + i, OWNERS)
        pl.semaphore_signal(
            sem, inc=1, device_id=(d // SEQ, lax.rem(d, SEQ)), device_id_type=MESH
        )
        return carry

    lax.fori_loop(1, OWNERS, body, 0)
    pl.semaphore_wait(sem, OWNERS - 1)


def remote(src, dst, send_sem, recv_sem, t, s):
    return pltpu.make_async_remote_copy(
        src_ref=src,
        dst_ref=dst,
        send_sem=send_sem,
        recv_sem=recv_sem,
        device_id=(t, s),
        device_id_type=MESH,
    )


def wait_bytes(ref, sem):
    pltpu.make_async_copy(ref, ref, sem).wait()


def unpack_rows(packed_ref, spread_buf, rows_buf):
    spread_buf[...] = packed_ref[...].astype(F32).reshape(OWNERS * PIECES, 128)
    for r in range(CAP):
        for q in range(WIDTH // 128):
            rows_buf[r * OWNERS : (r + 1) * OWNERS, q * 128 : (q + 1) * 128] = spread_buf[
                pl.ds(r * 4 + q, OWNERS, stride=PIECES), :
            ].astype(BF)


def query_block(core, k):
    return 2 * k + lax.rem(k + core, 2)


def query_core(s):
    return lax.rem((s + 1) // 2, 2)


def pack_rows(rows, count, spread_buf, out_ref, first):
    for r in range(CAP):
        for q in range(WIDTH // 128):
            spread_buf[pl.ds(r * 4 + q, count, stride=PIECES), :] = rows[
                r * count : (r + 1) * count, q * 128 : (q + 1) * 128
            ]
    chunk = spread_buf[: count * PIECES, :]
    out_ref[pl.ds(first, count)] = chunk.astype(BF).reshape(count, PIECES, 128)


def layer_kernel(
    ids_ref, stored_ref, len_ref, table_hbm, win_hbm, wo_hbm, cot_hbm,
    out_ref, grads_ref, want_ref,
    table_ref, win_ref, wo_ref, cot_ref, all_ids, ids2d, acc, outbuf, ans_ref,
    spread_buf, rows_buf, emb, norm_exact, in_spread, pre, gate, mixed_grad,
    qkv_send, qkv_all, key_nat, value_nat, key_t, value_t,
    o_send, o_all, attn_norm, d_send, d_all,
    dkv_acc, dkv_peer, dkv_send, dkv_all, dq_send, dq_all, qd_pad,
    load_sem, sem, qkv_sem, relay_sem, d_sem, peer_sem,
):
    t, s = places()
    me = t * SEQ + s
    core = lax.rem(t, 2)
    plane = t - core
    head_user = s // HEADS
    head = lax.rem(s, HEADS)
    owner_t = plane + head_user
    my_user = core
    my_core = query_core(s)
    my_slot = s // 2
    rows_dev = table_ref.shape[0]

    loads = [
        pltpu.make_async_copy(src, dst, load_sem.at[n])
        for n, (src, dst) in enumerate(
            ((table_hbm, table_ref), (win_hbm, win_ref), (wo_hbm, wo_ref), (cot_hbm, cot_ref))
        )
    ]
    for load in loads:
        load.start()
    all_ids[me] = ids_ref[...]
    barrier_all()

    def send(src, dst, send_sem, recv_sem, tt, ss):
        local = (tt == t) & (ss == s)

        @pl.when(local)
        def _():
            pltpu.make_async_copy(src, dst, recv_sem).start()

        @pl.when(jnp.logical_not(local))
        def _():
            remote(src, dst, send_sem, recv_sem, tt, ss).start()

    def sent(src, send_sem, tt, ss):
        @pl.when(jnp.logical_not((tt == t) & (ss == s)))
        def _():
            wait_bytes(src, send_sem)

    def to_plane(i, carry):
        ss = lax.rem(s + i, SEQ)
        remote(all_ids.at[me], all_ids.at[me], sem.at[10], sem.at[11], t, ss).start()
        return carry

    lax.fori_loop(1, SEQ, to_plane, 0)
    wait_bytes(all_ids.at[pl.ds(0, SEQ - 1)], sem.at[11])
    mine = all_ids.at[pl.ds(t * SEQ, SEQ)]

    def to_column(i, carry):
        tt = lax.rem(t + i, TABLE)
        remote(mine, mine, sem.at[12], sem.at[13], tt, s).start()
        return carry

    lax.fori_loop(1, TABLE, to_column, 0)

    stored = stored_ref[...]
    owner = stored // rows_dev
    owned = (iota((LEN, OWNERS), 1) == owner).astype(F32)
    earlier = (iota((LEN, LEN), 1) < iota((LEN, LEN), 0)).astype(BF)
    rank = jnp.sum(nn(earlier, owned.astype(BF)) * owned, axis=1, keepdims=True)
    slot = rank.astype(jnp.int32) * OWNERS + owner
    positions = s * LEN + iota((LEN, 1), 0)
    live = positions < len_ref[0]

    wait_bytes(all_ids.at[pl.ds(0, (TABLE - 1) * SEQ)], sem.at[13])

    def flat(b, carry):
        ids2d[pl.ds(b, 1), :] = all_ids[lax.rem(t * SEQ + b, OWNERS)]
        return carry

    lax.fori_loop(0, OWNERS, flat, 0, unroll=8)
    ids = ids2d[...]
    hit = ids // rows_dev == me
    local_row = lax.rem(ids, rows_dev).astype(F32)
    before = (iota((LEN, LEN), 0) < iota((LEN, LEN), 1)).astype(BF)
    order = nn(hit.astype(BF), before)
    value = jnp.where(hit, local_row + 1.0, 0.0)
    wanted = []
    for r in range(CAP):
        got = jnp.sum(jnp.where(order == r, value, 0.0), axis=1, keepdims=True) - 1.0
        wanted.append(got.astype(jnp.int32))
    lane = iota((OWNERS, OWNERS), 1)
    square = jnp.full((OWNERS, OWNERS), -1.0, F32)
    for r in range(CAP):
        square = jnp.where(lane == r, wanted[r].astype(F32), square)
    want_ref[...] = square.T[:8].astype(jnp.int32)

    block = 512
    half_count = OWNERS // 2
    loads[0].wait()

    def send_group(src_ref, dst_ref, dst_at, send_sem, recv_sem, g):
        tt = lax.rem(t + g, TABLE)

        def one(i, carry):
            ss = lax.rem(s + i, SEQ)

            @pl.when((g > 0) | (i > 0))
            def _():
                remote(
                    src_ref.at[g * SEQ + ss], dst_ref.at[dst_at(tt)], send_sem, recv_sem, tt, ss
                ).start()

            return carry

        lax.fori_loop(0, SEQ, one, 0)

    for half in range(2):
        low = half * half_count

        def gather(j, carry, low=low):
            base = j * block
            table_blk = table_ref[pl.ds(pl.multiple_of(base, block), block), :]
            cols = iota((half_count, block), 1) + base
            pick_rows = jnp.concatenate(
                [(w[low : low + half_count] == cols).astype(F32).astype(BF) for w in wanted], axis=0
            )
            part = nn(pick_rows, table_blk)

            @pl.when(j == 0)
            def _():
                acc[...] = part

            @pl.when(j > 0)
            def _():
                acc[...] += part

            return carry

        lax.fori_loop(0, rows_dev // block, gather, 0)
        pack_rows(acc, half_count, spread_buf, outbuf, low)

        def send_rows(g, carry):
            send_group(outbuf, ans_ref, lambda tt: me, sem.at[14], sem.at[15], g)
            return carry

        lax.fori_loop(half * TABLE // 2, (half + 1) * TABLE // 2, send_rows, 0)
    ans_ref[me] = outbuf[s]
    pick = (iota((LEN, CAP * OWNERS), 1) == slot).astype(F32).astype(BF)
    for load in loads[1:]:
        load.wait()
    cot = jnp.where(live, cot_ref[...].astype(F32), 0.0)
    mixed_grad[...] = nt(cot.astype(BF), wo_ref[...])
    dkv_acc[...] = jnp.zeros_like(dkv_acc)
    qd_pad[...] = jnp.zeros_like(qd_pad)
    wait_bytes(ans_ref.at[pl.ds(0, OWNERS - 1)], sem.at[15])

    unpack_rows(ans_ref, spread_buf, rows_buf)
    embedded = nn(pick, rows_buf[...])
    emb[...] = embedded
    normed, spread = normalize(embedded)
    norm_exact[...] = normed
    in_spread[...] = jnp.broadcast_to(spread, (LEN, 128))
    pre[...] = nn(normed.astype(BF), win_ref[...])
    for g in range(HEADS // 2):
        for part, (first, scale) in enumerate(((2, 0.0625), (3, 1.0), (1, 1.0))):
            low = first * WIDTH + g * 128
            act = silu(pre[:, low : low + 128]).astype(BF).astype(F32) * scale
            turned = act.T.astype(BF)
            qkv_send[2 * g, part * HD : (part + 1) * HD, :] = turned[:HD]
            qkv_send[2 * g + 1, part * HD : (part + 1) * HD, :] = turned[HD:]

    def send_qkv(i, carry):
        h = lax.rem(i + s, HEADS)
        send(
            qkv_send.at[h], qkv_all.at[s], sem.at[0], qkv_sem.at[my_slot],
            plane + my_core, my_user * HEADS + h,
        )
        return carry

    lax.fori_loop(0, HEADS, send_qkv, 0)

    gate[...] = silu(pre[:, :WIDTH])
    pre[...] = dsilu(pre[...])

    peer = plane + 1 - core

    def relay(k):
        i = query_block(core, k)
        wait_bytes(qkv_all.at[i], qkv_sem.at[k])
        ref = qkv_all.at[i, pl.ds(HD, 2 * HD)]
        remote(ref, ref, sem.at[1], relay_sem.at[k], peer, s).start()

    relay(0)

    def may_see(k):
        offset = lax.rem(k + core, 2) * LEN
        return iota((CHUNK, LEN), 0) <= iota((CHUNK, LEN), 1) + offset

    for k in range(CHUNKS):
        if k < CHUNKS - 1:
            relay(k + 1)
        wait_bytes(qkv_all.at[0, pl.ds(HD, 2 * HD)], relay_sem.at[k])
        for half in range(2):
            both = qkv_all[2 * k + half]
            rows = slice(half * LEN, (half + 1) * LEN)
            key_t[k, :, rows] = both[HD : 2 * HD]
            value_t[k, :, rows] = both[2 * HD :]
            key_nat[k, rows, :] = both[HD : 2 * HD].T
            value_nat[k, rows, :] = both[2 * HD :].T
        query = qkv_all[query_block(core, k), :HD]
        total = None
        for j in range(k + 1):
            u = nn(key_nat[j], query)
            if j == k:
                u = jnp.where(may_see(k), u, 0.0)
            part = nn(value_t[j], (u + u * jnp.tanh(u)).astype(BF))
            total = part if total is None else total + part
        o_send[k] = total
        send(
            o_send.at[k], o_all.at[head], sem.at[2], sem.at[3],
            owner_t, query_block(core, k),
        )

    wait_bytes(o_all, sem.at[3])
    attention = o_all[...].reshape(WIDTH, LEN).T
    attention = jnp.where(live, attention, 0.0)
    attn, attn_spread = normalize(attention)
    attn_norm[...] = attn
    dz = mixed_grad[...] * gate[...]
    attention_grad = norm_back(dz, attn, attn_spread).astype(BF).astype(F32)
    d_send[...] = (0.5 * attention_grad).T.astype(BF).reshape(HEADS, HD, LEN)

    def send_d(i, carry):
        h = lax.rem(i + s, HEADS)
        send(
            d_send.at[h], d_all.at[my_slot], sem.at[4], d_sem.at[my_slot],
            plane + my_core, my_user * HEADS + h,
        )
        return carry

    lax.fori_loop(0, HEADS, send_d, 0)
    mixed = (attn * gate[...]).astype(BF)
    branch = nn(mixed, wo_ref[...])
    out_ref[...] = jnp.where(live, emb[...] + branch, 0.0).astype(BF)

    def reduce_keys(k):
        wait_bytes(dkv_peer.at[k], peer_sem.at[k])
        half = lax.rem(k + core, 2)
        own = dkv_acc[k, pl.ds(pl.multiple_of(half * LEN, LEN), LEN), :]
        dkv_send[k] = (2.0 * (own + dkv_peer[k])).astype(BF)
        send(
            dkv_send.at[k], dkv_all.at[head], sem.at[5], sem.at[6],
            owner_t, query_block(core, k),
        )

    def peer_half(k):
        half = 1 - lax.rem(k + core, 2)
        return dkv_acc.at[k, pl.ds(pl.multiple_of(half * LEN, LEN), LEN)]

    for k in range(CHUNKS - 1, -1, -1):
        wait_bytes(d_all.at[k], d_sem.at[k])
        query = qkv_all[query_block(core, k), :HD]
        grad = d_all[k]
        qd_pad[:LEN, :HD] = query.T
        qd_pad[LEN:, HD:] = grad.T
        pair = qd_pad[...]
        total = None
        for j in range(k + 1):
            u = nn(key_nat[j], query)
            dp = nn(value_nat[j], grad)
            th = jnp.tanh(u)
            a = 1.0 + th
            p = u * a
            ds = dp * (a * (1.0 + u * (1.0 - th)))
            if j == k:
                p = jnp.where(may_see(k), p, 0.0)
                ds = jnp.where(may_see(k), ds, 0.0)
            p = p.astype(BF)
            ds = ds.astype(BF)
            dkv_acc[j] += nn(ds, pair[:LEN]) + nn(p, pair[LEN:])
            part = nn(key_t[j], ds)
            total = part if total is None else total + part
        dq_send[k] = (0.125 * total).astype(BF)
        send(
            dq_send.at[k], dq_all.at[head], sem.at[7], sem.at[8],
            owner_t, query_block(core, k),
        )
        remote(peer_half(k), dkv_peer.at[k], sem.at[9], peer_sem.at[k], peer, s).start()
        if k < CHUNKS - 1:
            reduce_keys(k + 1)
    reduce_keys(0)

    def back(first, gradient):
        cols = slice(first * WIDTH, (first + 1) * WIDTH)
        return nt((gradient * pre[:, cols]).astype(BF), win_ref[:, cols])

    def by_head(low):
        return jnp.concatenate(
            [dkv_all[h][:, low : low + HD].astype(F32) for h in range(HEADS)], axis=1
        )

    norm_grad = back(0, mixed_grad[...] * attn_norm[...])
    wait_bytes(dq_all, sem.at[8])
    norm_grad += back(2, dq_all[...].reshape(WIDTH, LEN).astype(F32).T)
    wait_bytes(dkv_all, sem.at[6])
    norm_grad += back(1, by_head(HD))
    norm_grad += back(3, by_head(0))
    cot = jnp.where(live, cot_ref[...].astype(F32), 0.0)
    embed_grad = cot + norm_back(norm_grad, norm_exact[...], in_spread[:, :1])
    wait_bytes(outbuf.at[pl.ds(0, OWNERS - 1)], sem.at[14])
    turned_owner = lax.rem(owner + (OWNERS - t * SEQ), OWNERS)
    turned_slot = rank.astype(jnp.int32) * OWNERS + turned_owner
    put_pick = (iota((LEN, CAP * OWNERS), 1) == turned_slot).astype(F32).astype(BF)
    acc_put = lax.dot_general(
        put_pick, embed_grad.astype(BF), (((0,), (0,)), ((), ())), preferred_element_type=F32
    )
    pack_rows(acc_put, OWNERS, spread_buf, outbuf, 0)

    def send_grads(g, carry):
        send_group(
            outbuf, grads_ref, lambda tt: lax.rem(t - tt + TABLE, TABLE) * SEQ + s,
            sem.at[16], sem.at[17], g,
        )
        return carry

    lax.fori_loop(0, TABLE, send_grads, 0)
    grads_ref[s] = outbuf[s]

    wait_bytes(all_ids.at[pl.ds(0, SEQ - 1)], sem.at[10])
    wait_bytes(all_ids.at[pl.ds(0, (TABLE - 1) * SEQ)], sem.at[12])

    def drain(i, carry):
        sent(qkv_send.at[0], sem.at[0], plane + my_core, my_user * HEADS + i)
        sent(d_send.at[0], sem.at[4], plane + my_core, my_user * HEADS + i)
        wait_bytes(qkv_all.at[0, pl.ds(HD, 2 * HD)], sem.at[1])
        wait_bytes(dkv_peer.at[0], sem.at[9])
        block_now = query_block(core, i)
        sent(o_send.at[0], sem.at[2], owner_t, block_now)
        sent(dkv_send.at[0], sem.at[5], owner_t, block_now)
        sent(dq_send.at[0], sem.at[7], owner_t, block_now)
        return carry

    lax.fori_loop(0, CHUNKS, drain, 0)
    wait_bytes(grads_ref.at[pl.ds(0, OWNERS - 1)], sem.at[17])
    wait_bytes(outbuf.at[pl.ds(0, OWNERS - 1)], sem.at[16])


def layer(stored, length, item_table, input_proj, output_proj, cot):
    anywhere = pl.BlockSpec(memory_space=pl.ANY)
    return pl.pallas_call(
        layer_kernel,
        out_shape=(
            jax.ShapeDtypeStruct((LEN, WIDTH), BF),
            jax.ShapeDtypeStruct((OWNERS, PIECES, 128), BF),
            jax.ShapeDtypeStruct((8, OWNERS), jnp.int32),
        ),
        in_specs=[VM, VM, SM, anywhere, anywhere, anywhere, anywhere],
        out_specs=(VM, VM, VM),
        scratch_shapes=[
            pltpu.VMEM(item_table.shape, BF),
            pltpu.VMEM((WIDTH, 4 * WIDTH), BF),
            pltpu.VMEM((WIDTH, WIDTH), BF),
            pltpu.VMEM((LEN, WIDTH), BF),
            pltpu.VMEM((OWNERS, 1, LEN), jnp.int32),
            pltpu.VMEM((OWNERS, LEN), jnp.int32),
            pltpu.VMEM((CAP * OWNERS // 2, WIDTH), F32),
            pltpu.VMEM((OWNERS, PIECES, 128), BF),
            pltpu.VMEM((OWNERS, PIECES, 128), BF),
            pltpu.VMEM((OWNERS * PIECES, 128), F32),
            pltpu.VMEM((CAP * OWNERS, WIDTH), BF),
            pltpu.VMEM((LEN, WIDTH), F32),
            pltpu.VMEM((LEN, WIDTH), F32),
            pltpu.VMEM((LEN, 128), F32),
            pltpu.VMEM((LEN, 4 * WIDTH), F32),
            pltpu.VMEM((LEN, WIDTH), F32),
            pltpu.VMEM((LEN, WIDTH), F32),
            pltpu.VMEM((HEADS, 3 * HD, LEN), BF),
            pltpu.VMEM((SEQ, 3 * HD, LEN), BF),
            pltpu.VMEM((CHUNKS, CHUNK, HD), BF),
            pltpu.VMEM((CHUNKS, CHUNK, HD), BF),
            pltpu.VMEM((CHUNKS, HD, CHUNK), BF),
            pltpu.VMEM((CHUNKS, HD, CHUNK), BF),
            pltpu.VMEM((CHUNKS, HD, LEN), F32),
            pltpu.VMEM((HEADS, HD, LEN), F32),
            pltpu.VMEM((LEN, WIDTH), F32),
            pltpu.VMEM((HEADS, HD, LEN), BF),
            pltpu.VMEM((CHUNKS, HD, LEN), BF),
            pltpu.VMEM((CHUNKS, CHUNK, 2 * HD), F32),
            pltpu.VMEM((CHUNKS, LEN, 2 * HD), F32),
            pltpu.VMEM((CHUNKS, LEN, 2 * HD), BF),
            pltpu.VMEM((HEADS, LEN, 2 * HD), BF),
            pltpu.VMEM((CHUNKS, HD, LEN), BF),
            pltpu.VMEM((HEADS, HD, LEN), BF),
            pltpu.VMEM((2 * LEN, 2 * HD), BF),
            pltpu.SemaphoreType.DMA((4,)),
            pltpu.SemaphoreType.DMA((18,)),
            pltpu.SemaphoreType.DMA((CHUNKS,)),
            pltpu.SemaphoreType.DMA((CHUNKS,)),
            pltpu.SemaphoreType.DMA((CHUNKS,)),
            pltpu.SemaphoreType.DMA((CHUNKS,)),
        ],
        compiler_params=pltpu.CompilerParams(
            collective_id=0, has_side_effects=True, vmem_limit_bytes=VMEM_LIMIT
        ),
        name="layer",
    )(stored[None, :], stored[:, None], length, item_table, input_proj, output_proj, cot)


def sum_kernel(block, want_ref, packed_ref, out_ref, spread_buf, rows_buf):
    j = pl.program_id(0)

    @pl.when(j == 0)
    def _():
        unpack_rows(packed_ref, spread_buf, rows_buf)

    rows = iota((block, OWNERS), 0) + j * block
    pick = jnp.concatenate(
        [(want_ref[r : r + 1, :] == rows).astype(F32).astype(BF) for r in range(CAP)], axis=1
    )
    out_ref[...] = nn(pick, rows_buf[...]).astype(BF)


def sum_rows(wanted, arrived, rows_dev):
    block = 512
    return pl.pallas_call(
        functools.partial(sum_kernel, block),
        out_shape=jax.ShapeDtypeStruct((rows_dev, WIDTH), BF),
        grid=(rows_dev // block,),
        in_specs=[
            pl.BlockSpec((8, OWNERS), lambda j: (0, 0)),
            pl.BlockSpec((OWNERS, PIECES, 128), lambda j: (0, 0, 0)),
        ],
        out_specs=pl.BlockSpec((block, WIDTH), lambda j: (j, 0)),
        scratch_shapes=[
            pltpu.VMEM((OWNERS * PIECES, 128), F32),
            pltpu.VMEM((CAP * OWNERS, WIDTH), BF),
        ],
        compiler_params=pltpu.CompilerParams(vmem_limit_bytes=VMEM_LIMIT),
        name="sums",
    )(wanted, arrived)


def local(item_ids, history_len, row_place, item_table, input_proj, output_proj, out_cotangent):
    stored = row_place[item_ids[0]]
    layer_out, arrived, wanted = layer(
        stored, history_len, item_table, input_proj, output_proj, out_cotangent[0]
    )
    table_grad = sum_rows(wanted, arrived, item_table.shape[0])
    return layer_out[None], table_grad


def solution(mesh):
    placed = (
        P("table", "seq"),
        P("table"),
        P(),
        P(("table", "seq"), None),
        P(),
        P(),
        P("table", "seq", None),
    )
    return jax.shard_map(
        local,
        mesh=mesh,
        in_specs=placed,
        out_specs=(P("table", "seq", None), P(("table", "seq"), None)),
        check_vma=False,
    )
```

```python
import functools

import jax
import jax.numpy as jnp
from jax import lax
from jax.experimental import pallas as pl
from jax.experimental.pallas import tpu as pltpu
from jax.sharding import PartitionSpec as P

HEADS = 8
CAP = 6
EPS = 1e-05
F32 = jnp.float32
BF = jnp.bfloat16
MESH = pl.DeviceIdType.MESH
VM = pl.BlockSpec(memory_space=pltpu.VMEM)
SM = pl.BlockSpec(memory_space=pltpu.SMEM)
TABLE, SEQ = 8, 16
OWNERS = TABLE * SEQ
LEN = 256
HD = 64
WIDTH = 512
PIECES = CAP * WIDTH // 128
CHUNK = 2 * LEN
CHUNKS = SEQ // 2
AHEAD = 3
VMEM_LIMIT = 56 * 2**20


def nn(a, b):
    return lax.dot_general(a, b, (((1,), (0,)), ((), ())), preferred_element_type=F32)


def nt(a, b):
    return lax.dot_general(a, b, (((1,), (1,)), ((), ())), preferred_element_type=F32)


def iota(shape, dim):
    return lax.broadcasted_iota(jnp.int32, shape, dim)


def silu(x):
    u = 0.5 * x
    return u + u * jnp.tanh(u)


def dsilu(x):
    u = 0.5 * x
    th = jnp.tanh(u)
    return (0.5 + 0.5 * th) * (1.0 + u * (1.0 - th))


def normalize(x, axis=1):
    def mean(y):
        return jnp.mean(y, axis=axis, keepdims=True)

    centred = x - mean(x)
    spread = jnp.sqrt(mean(centred * centred) + EPS)
    return centred / spread, spread


def norm_back(gradient, normed, spread, axis=1):
    def mean(y):
        return jnp.mean(y, axis=axis, keepdims=True)

    return (gradient - mean(gradient) - normed * mean(gradient * normed)) / spread


def places():
    t = lax.axis_index("table")
    s = lax.axis_index("seq")
    return t, s


def barrier_all():
    t, s = places()
    me = t * SEQ + s
    sem = pltpu.get_barrier_semaphore()

    def body(i, carry):
        d = lax.rem(me + i, OWNERS)
        pl.semaphore_signal(
            sem, inc=1, device_id=(d // SEQ, lax.rem(d, SEQ)), device_id_type=MESH
        )
        return carry

    lax.fori_loop(1, OWNERS, body, 0)
    pl.semaphore_wait(sem, OWNERS - 1)


def remote(src, dst, send_sem, recv_sem, t, s):
    return pltpu.make_async_remote_copy(
        src_ref=src,
        dst_ref=dst,
        send_sem=send_sem,
        recv_sem=recv_sem,
        device_id=(t, s),
        device_id_type=MESH,
    )


def wait_bytes(ref, sem):
    pltpu.make_async_copy(ref, ref, sem).wait()


def unpack_rows(packed_ref, spread_buf, rows_buf):
    spread_buf[...] = packed_ref[...].astype(F32).reshape(OWNERS * PIECES, 128)
    for r in range(CAP):
        for q in range(WIDTH // 128):
            rows_buf[r * OWNERS : (r + 1) * OWNERS, q * 128 : (q + 1) * 128] = spread_buf[
                pl.ds(r * 4 + q, OWNERS, stride=PIECES), :
            ].astype(BF)


def query_block(core, k):
    return 2 * k + lax.rem(k + core, 2)


def query_core(s):
    return lax.rem((s + 1) // 2, 2)


def pack_rows(rows, count, spread_buf, out_ref, first):
    for r in range(CAP):
        for q in range(WIDTH // 128):
            spread_buf[pl.ds(r * 4 + q, count, stride=PIECES), :] = rows[
                r * count : (r + 1) * count, q * 128 : (q + 1) * 128
            ]
    chunk = spread_buf[: count * PIECES, :]
    out_ref[pl.ds(first, count)] = chunk.astype(BF).reshape(count, PIECES, 128)


def layer_kernel(
    ids_ref, len_ref, table_hbm, win_hbm, wo_hbm, cot_hbm,
    out_ref, grads_ref, want_ref,
    table_ref, win_ref, wo_ref, cot_ref, all_ids, ids2d, acc, outbuf, ans_ref,
    spread_buf, rows_buf, emb, norm_exact, in_spread, pre, gate, mixed_grad,
    qkv_send, qkv_all, key_nat, value_nat, key_t, value_t,
    o_send, o_all, attn_norm, d_send, d_all,
    dkv_acc, dkv_peer, dkv_send, dkv_all, dq_send, dq_all, qd_pad, p_ahead, c_ahead,
    load_sem, sem, qkv_sem, relay_sem, d_sem, peer_sem,
):
    t, s = places()
    me = t * SEQ + s
    core = lax.rem(t, 2)
    plane = t - core
    head_user = s // HEADS
    head = lax.rem(s, HEADS)
    owner_t = plane + head_user
    my_user = core
    my_core = query_core(s)
    my_slot = s // 2
    rows_dev = table_ref.shape[0]

    loads = [
        pltpu.make_async_copy(src, dst, load_sem.at[n])
        for n, (src, dst) in enumerate(
            ((table_hbm, table_ref), (win_hbm, win_ref), (wo_hbm, wo_ref), (cot_hbm, cot_ref))
        )
    ]
    for load in loads:
        load.start()
    all_ids[me] = ids_ref[...]
    barrier_all()

    def send(src, dst, send_sem, recv_sem, tt, ss):
        local = (tt == t) & (ss == s)

        @pl.when(local)
        def _():
            pltpu.make_async_copy(src, dst, recv_sem).start()

        @pl.when(jnp.logical_not(local))
        def _():
            remote(src, dst, send_sem, recv_sem, tt, ss).start()

    def sent(src, send_sem, tt, ss):
        @pl.when(jnp.logical_not((tt == t) & (ss == s)))
        def _():
            wait_bytes(src, send_sem)

    def to_plane(i, carry):
        ss = lax.rem(s + i, SEQ)
        remote(all_ids.at[me], all_ids.at[me], sem.at[10], sem.at[11], t, ss).start()
        return carry

    lax.fori_loop(1, SEQ, to_plane, 0)
    wait_bytes(all_ids.at[pl.ds(0, SEQ - 1)], sem.at[11])
    mine = all_ids.at[pl.ds(t * SEQ, SEQ)]

    def to_column(i, carry):
        tt = lax.rem(t + i, TABLE)
        remote(mine, mine, sem.at[12], sem.at[13], tt, s).start()
        return carry

    lax.fori_loop(1, TABLE, to_column, 0)

    diagonal = iota((LEN, LEN), 0) == iota((LEN, LEN), 1)
    stored = jnp.sum(
        jnp.where(diagonal, ids_ref[...].astype(F32), 0.0), axis=1, keepdims=True
    ).astype(jnp.int32)
    owner = stored // rows_dev
    owned = (iota((LEN, OWNERS), 1) == owner).astype(F32)
    earlier = (iota((LEN, LEN), 1) < iota((LEN, LEN), 0)).astype(BF)
    rank = jnp.sum(nn(earlier, owned.astype(BF)) * owned, axis=1, keepdims=True)
    slot = rank.astype(jnp.int32) * OWNERS + owner
    positions = s * LEN + iota((LEN, 1), 0)
    live = positions < len_ref[0]

    wait_bytes(all_ids.at[pl.ds(0, (TABLE - 1) * SEQ)], sem.at[13])

    def flat(b, carry):
        ids2d[pl.ds(b, 1), :] = all_ids[lax.rem(t * SEQ + b, OWNERS)]
        return carry

    lax.fori_loop(0, OWNERS, flat, 0, unroll=8)
    ids = ids2d[...]
    hit = ids // rows_dev == me
    local_row = lax.rem(ids, rows_dev).astype(F32)
    before = (iota((LEN, LEN), 0) < iota((LEN, LEN), 1)).astype(BF)
    order = nn(hit.astype(BF), before)
    value = jnp.where(hit, local_row + 1.0, 0.0)
    wanted = []
    for r in range(CAP):
        got = jnp.sum(jnp.where(order == r, value, 0.0), axis=1, keepdims=True) - 1.0
        wanted.append(got.astype(jnp.int32))
    lane = iota((OWNERS, OWNERS), 1)
    square = jnp.full((OWNERS, OWNERS), -1.0, F32)
    for r in range(CAP):
        square = jnp.where(lane == r, wanted[r].astype(F32), square)
    want_ref[...] = square.T[:8].astype(jnp.int32)

    block = 512
    half_count = OWNERS // 2
    loads[0].wait()

    def send_one(src_ref, dst_ref, dst_at, send_sem, recv_sem, n):
        tt = lax.rem(t + n // SEQ, TABLE)
        ss = lax.rem(s + n, SEQ)
        remote(
            src_ref.at[n // SEQ * SEQ + ss], dst_ref.at[dst_at(tt)], send_sem, recv_sem, tt, ss
        ).start()

    def send_row(n):
        send_one(outbuf, ans_ref, lambda tt: me, sem.at[14], sem.at[15], n)

    steps = rows_dev // block
    each = half_count // steps
    for half in range(2):
        low = half * half_count

        def gather(j, carry, half=half, low=low):
            base = j * block
            table_blk = table_ref[pl.ds(pl.multiple_of(base, block), block), :]
            cols = iota((half_count, block), 1) + base
            pick_rows = jnp.concatenate(
                [(w[low : low + half_count] == cols).astype(F32).astype(BF) for w in wanted], axis=0
            )
            if half:
                for n in range(1, each):
                    send_row(j * each + n)
            part = nn(pick_rows, table_blk)
            acc[...] += part
            return carry

        acc[...] = jnp.zeros_like(acc)
        lax.fori_loop(0, steps, gather, 0)
        pack_rows(acc, half_count, spread_buf, outbuf, low)

    def send_rest(n, carry):
        send_row(half_count + n)
        return carry

    lax.fori_loop(0, half_count, send_rest, 0)
    for n in range(1, steps):
        send_row(n * each)
    ans_ref[me] = outbuf[s]
    pick = (iota((LEN, CAP * OWNERS), 1) == slot).astype(F32).astype(BF)
    for load in loads[1:]:
        load.wait()
    cot = jnp.where(live, cot_ref[...].astype(F32), 0.0)
    mixed_grad[...] = nt(wo_ref[...], cot.astype(BF))
    dkv_acc[...] = jnp.zeros_like(dkv_acc)
    qd_pad[...] = jnp.zeros_like(qd_pad)
    wait_bytes(ans_ref.at[pl.ds(0, OWNERS - 1)], sem.at[15])

    unpack_rows(ans_ref, spread_buf, rows_buf)
    embedded = nn(pick, rows_buf[...])
    emb[...] = embedded
    normed, spread = normalize(embedded)
    norm_exact[...] = normed
    in_spread[...] = jnp.broadcast_to(spread, (LEN, 128))
    pre[...] = nn(normed.astype(BF), win_ref[...])
    for g in range(HEADS // 2):
        for part, (first, scale) in enumerate(((2, 0.0625), (3, 1.0), (1, 1.0))):
            low = first * WIDTH + g * 128
            act = silu(pre[:, low : low + 128]).astype(BF).astype(F32) * scale
            turned = act.T.astype(BF)
            qkv_send[2 * g, part * HD : (part + 1) * HD, :] = turned[:HD]
            qkv_send[2 * g + 1, part * HD : (part + 1) * HD, :] = turned[HD:]

    def send_qkv(i, carry):
        h = lax.rem(i + s, HEADS)
        send(
            qkv_send.at[h], qkv_all.at[s], sem.at[0], qkv_sem.at[my_slot],
            plane + my_core, my_user * HEADS + h,
        )
        return carry

    lax.fori_loop(0, HEADS, send_qkv, 0)

    gate[...] = silu(pre[:, :WIDTH]).T
    pre[...] = dsilu(pre[...])

    peer = plane + 1 - core

    def relay(k):
        i = query_block(core, k)
        wait_bytes(qkv_all.at[i], qkv_sem.at[k])
        ref = qkv_all.at[i, pl.ds(HD, 2 * HD)]
        remote(ref, ref, sem.at[1], relay_sem.at[k], peer, s).start()

    for k in range(AHEAD):
        relay(k)

    def may_see(k):
        offset = lax.rem(k + core, 2) * LEN
        return iota((CHUNK, LEN), 0) <= iota((CHUNK, LEN), 1) + offset

    for k in range(CHUNKS):
        if k + AHEAD < CHUNKS:
            relay(k + AHEAD)
        wait_bytes(qkv_all.at[0, pl.ds(HD, 2 * HD)], relay_sem.at[k])
        for half in range(2):
            both = qkv_all[2 * k + half]
            rows = slice(half * LEN, (half + 1) * LEN)
            key_t[k, :, rows] = both[HD : 2 * HD]
            value_t[k, :, rows] = both[2 * HD :]
            key_nat[k, rows, :] = both[HD : 2 * HD].T
            value_nat[k, rows, :] = both[2 * HD :].T
        query = qkv_all[query_block(core, k), :HD]
        total = None
        for j in range(k + 1):
            u = nn(key_nat[j], query)
            if j == k:
                u = jnp.where(may_see(k), u, 0.0)
            part = nn(value_t[j], (u + u * jnp.tanh(u)).astype(BF))
            total = part if total is None else total + part
        o_send[k] = total
        send(
            o_send.at[k], o_all.at[head], sem.at[2], sem.at[3],
            owner_t, query_block(core, k),
        )

    def score_terms(k, j):
        u = nn(key_nat[j], qkv_all[query_block(core, k), :HD])
        th = jnp.tanh(u)
        a = 1.0 + th
        p = u * a
        c = a * (1.0 + u * (1.0 - th))
        if j == k:
            p = jnp.where(may_see(k), p, 0.0)
            c = jnp.where(may_see(k), c, 0.0)
        return p.astype(BF), c

    def score_ahead(k):
        for j in range(k + 1):
            p, c = score_terms(k, j)
            p_ahead[CHUNKS - 1 - k, j] = p
            c_ahead[CHUNKS - 1 - k, j] = c

    score_ahead(CHUNKS - 1)

    wait_bytes(o_all, sem.at[3])
    attention = o_all[...].reshape(WIDTH, LEN)
    live_lanes = s * LEN + iota((1, LEN), 1) < len_ref[0]
    attention = jnp.where(live_lanes, attention, 0.0)
    attn, attn_spread = normalize(attention, 0)
    attn_norm[...] = attn
    dz = mixed_grad[...] * gate[...]
    attention_grad = norm_back(dz, attn, attn_spread, 0).astype(BF).astype(F32)
    d_send[...] = (0.5 * attention_grad).astype(BF).reshape(HEADS, HD, LEN)

    def send_d(i, carry):
        h = lax.rem(i + s, HEADS)
        send(
            d_send.at[h], d_all.at[my_slot], sem.at[4], d_sem.at[my_slot],
            plane + my_core, my_user * HEADS + h,
        )
        return carry

    lax.fori_loop(0, HEADS, send_d, 0)
    mixed = (attn_norm[...] * gate[...]).T.astype(BF)
    branch = nn(mixed, wo_ref[...])
    out_ref[...] = jnp.where(live, emb[...] + branch, 0.0).astype(BF)

    score_ahead(CHUNKS - 2)

    def reduce_keys(k):
        wait_bytes(dkv_peer.at[k], peer_sem.at[k])
        half = lax.rem(k + core, 2)
        own = dkv_acc[k, pl.ds(pl.multiple_of(half * LEN, LEN), LEN), :]
        dkv_send[k] = (2.0 * (own + dkv_peer[k])).astype(BF)
        send(
            dkv_send.at[k], dkv_all.at[head], sem.at[5], sem.at[6],
            owner_t, query_block(core, k),
        )

    def peer_half(k):
        half = 1 - lax.rem(k + core, 2)
        return dkv_acc.at[k, pl.ds(pl.multiple_of(half * LEN, LEN), LEN)]

    for k in range(CHUNKS - 1, -1, -1):
        wait_bytes(d_all.at[k], d_sem.at[k])
        query = qkv_all[query_block(core, k), :HD]
        grad = d_all[k]
        qd_pad[:LEN, :HD] = query.T
        qd_pad[LEN:, HD:] = grad.T
        pair = qd_pad[...]
        total = None
        for j in range(k + 1):
            if k >= CHUNKS - 2:
                p, c = p_ahead[CHUNKS - 1 - k, j], c_ahead[CHUNKS - 1 - k, j]
            else:
                p, c = score_terms(k, j)
            ds = (nn(value_nat[j], grad) * c).astype(BF)
            dkv_acc[j] += nn(ds, pair[:LEN]) + nn(p, pair[LEN:])
            part = nn(key_t[j], ds)
            total = part if total is None else total + part
        dq_send[k] = (0.125 * total).astype(BF)
        send(
            dq_send.at[k], dq_all.at[head], sem.at[7], sem.at[8],
            owner_t, query_block(core, k),
        )
        remote(peer_half(k), dkv_peer.at[k], sem.at[9], peer_sem.at[k], peer, s).start()
        if k < CHUNKS - 1:
            reduce_keys(k + 1)
    reduce_keys(0)

    def back(first, gradient):
        cols = slice(first * WIDTH, (first + 1) * WIDTH)
        return nt((gradient * pre[:, cols]).astype(BF), win_ref[:, cols])

    def by_head(low):
        return jnp.concatenate(
            [dkv_all[h][:, low : low + HD].astype(F32) for h in range(HEADS)], axis=1
        )

    norm_grad = back(0, (mixed_grad[...] * attn_norm[...]).T)
    wait_bytes(dq_all, sem.at[8])
    norm_grad += back(2, dq_all[...].reshape(WIDTH, LEN).astype(F32).T)
    wait_bytes(dkv_all, sem.at[6])
    norm_grad += back(1, by_head(HD))
    norm_grad += back(3, by_head(0))
    cot = jnp.where(live, cot_ref[...].astype(F32), 0.0)
    embed_grad = cot + norm_back(norm_grad, norm_exact[...], in_spread[:, :1])
    wait_bytes(outbuf.at[pl.ds(0, OWNERS - 1)], sem.at[14])
    turned_owner = lax.rem(owner + (OWNERS - t * SEQ), OWNERS)
    turned_slot = rank.astype(jnp.int32) * OWNERS + turned_owner
    put_pick = (iota((LEN, CAP * OWNERS), 1) == turned_slot).astype(F32).astype(BF)
    acc_put = lax.dot_general(
        put_pick, embed_grad.astype(BF), (((0,), (0,)), ((), ())), preferred_element_type=F32
    )
    pack_rows(acc_put, OWNERS, spread_buf, outbuf, 0)

    def send_grads(n, carry):
        send_one(
            outbuf, grads_ref, lambda tt: lax.rem(t - tt + TABLE, TABLE) * SEQ + s,
            sem.at[16], sem.at[17], n,
        )
        return carry

    lax.fori_loop(1, OWNERS, send_grads, 0)
    grads_ref[s] = outbuf[s]

    wait_bytes(all_ids.at[pl.ds(0, SEQ - 1)], sem.at[10])
    wait_bytes(all_ids.at[pl.ds(0, (TABLE - 1) * SEQ)], sem.at[12])

    def drain(i, carry):
        sent(qkv_send.at[0], sem.at[0], plane + my_core, my_user * HEADS + i)
        sent(d_send.at[0], sem.at[4], plane + my_core, my_user * HEADS + i)
        wait_bytes(qkv_all.at[0, pl.ds(HD, 2 * HD)], sem.at[1])
        wait_bytes(dkv_peer.at[0], sem.at[9])
        block_now = query_block(core, i)
        sent(o_send.at[0], sem.at[2], owner_t, block_now)
        sent(dkv_send.at[0], sem.at[5], owner_t, block_now)
        sent(dq_send.at[0], sem.at[7], owner_t, block_now)
        return carry

    lax.fori_loop(0, CHUNKS, drain, 0)
    wait_bytes(grads_ref.at[pl.ds(0, OWNERS - 1)], sem.at[17])
    wait_bytes(outbuf.at[pl.ds(0, OWNERS - 1)], sem.at[16])


def layer(stored, length, item_table, input_proj, output_proj, cot):
    anywhere = pl.BlockSpec(memory_space=pl.ANY)
    return pl.pallas_call(
        layer_kernel,
        out_shape=(
            jax.ShapeDtypeStruct((LEN, WIDTH), BF),
            jax.ShapeDtypeStruct((OWNERS, PIECES, 128), BF),
            jax.ShapeDtypeStruct((8, OWNERS), jnp.int32),
        ),
        in_specs=[VM, SM, anywhere, anywhere, anywhere, anywhere],
        out_specs=(VM, VM, VM),
        scratch_shapes=[
            pltpu.VMEM(item_table.shape, BF),
            pltpu.VMEM((WIDTH, 4 * WIDTH), BF),
            pltpu.VMEM((WIDTH, WIDTH), BF),
            pltpu.VMEM((LEN, WIDTH), BF),
            pltpu.VMEM((OWNERS, 1, LEN), jnp.int32),
            pltpu.VMEM((OWNERS, LEN), jnp.int32),
            pltpu.VMEM((CAP * OWNERS // 2, WIDTH), F32),
            pltpu.VMEM((OWNERS, PIECES, 128), BF),
            pltpu.VMEM((OWNERS, PIECES, 128), BF),
            pltpu.VMEM((OWNERS * PIECES, 128), F32),
            pltpu.VMEM((CAP * OWNERS, WIDTH), BF),
            pltpu.VMEM((LEN, WIDTH), F32),
            pltpu.VMEM((LEN, WIDTH), F32),
            pltpu.VMEM((LEN, 128), F32),
            pltpu.VMEM((LEN, 4 * WIDTH), F32),
            pltpu.VMEM((WIDTH, LEN), F32),
            pltpu.VMEM((WIDTH, LEN), F32),
            pltpu.VMEM((HEADS, 3 * HD, LEN), BF),
            pltpu.VMEM((SEQ, 3 * HD, LEN), BF),
            pltpu.VMEM((CHUNKS, CHUNK, HD), BF),
            pltpu.VMEM((CHUNKS, CHUNK, HD), BF),
            pltpu.VMEM((CHUNKS, HD, CHUNK), BF),
            pltpu.VMEM((CHUNKS, HD, CHUNK), BF),
            pltpu.VMEM((CHUNKS, HD, LEN), F32),
            pltpu.VMEM((HEADS, HD, LEN), F32),
            pltpu.VMEM((WIDTH, LEN), F32),
            pltpu.VMEM((HEADS, HD, LEN), BF),
            pltpu.VMEM((CHUNKS, HD, LEN), BF),
            pltpu.VMEM((CHUNKS, CHUNK, 2 * HD), F32),
            pltpu.VMEM((CHUNKS, LEN, 2 * HD), F32),
            pltpu.VMEM((CHUNKS, LEN, 2 * HD), BF),
            pltpu.VMEM((HEADS, LEN, 2 * HD), BF),
            pltpu.VMEM((CHUNKS, HD, LEN), BF),
            pltpu.VMEM((HEADS, HD, LEN), BF),
            pltpu.VMEM((2 * LEN, 2 * HD), BF),
            pltpu.VMEM((2, CHUNKS, CHUNK, LEN), BF),
            pltpu.VMEM((2, CHUNKS, CHUNK, LEN), F32),
            pltpu.SemaphoreType.DMA((4,)),
            pltpu.SemaphoreType.DMA((18,)),
            pltpu.SemaphoreType.DMA((CHUNKS,)),
            pltpu.SemaphoreType.DMA((CHUNKS,)),
            pltpu.SemaphoreType.DMA((CHUNKS,)),
            pltpu.SemaphoreType.DMA((CHUNKS,)),
        ],
        compiler_params=pltpu.CompilerParams(
            collective_id=0, has_side_effects=True, vmem_limit_bytes=VMEM_LIMIT
        ),
        name="layer",
    )(stored[None, :], length, item_table, input_proj, output_proj, cot)


def sum_kernel(block, want_ref, packed_ref, layer_ref, out_ref, same_ref, spread_buf, rows_buf):
    j = pl.program_id(0)

    @pl.when(j == 0)
    def _():
        unpack_rows(packed_ref, spread_buf, rows_buf)

    same_ref[...] = layer_ref[...]
    rows = iota((block, OWNERS), 0) + j * block
    pick = jnp.concatenate(
        [(want_ref[r : r + 1, :] == rows).astype(F32).astype(BF) for r in range(CAP)], axis=1
    )
    out_ref[...] = nn(pick, rows_buf[...]).astype(BF)


def sum_rows(wanted, arrived, layer_out, rows_dev):
    block = 512
    part = LEN * block // rows_dev
    return pl.pallas_call(
        functools.partial(sum_kernel, block),
        out_shape=(
            jax.ShapeDtypeStruct((rows_dev, WIDTH), BF),
            jax.ShapeDtypeStruct((LEN, WIDTH), BF),
        ),
        grid=(rows_dev // block,),
        in_specs=[
            pl.BlockSpec((8, OWNERS), lambda j: (0, 0)),
            pl.BlockSpec((OWNERS, PIECES, 128), lambda j: (0, 0, 0)),
            pl.BlockSpec((part, WIDTH), lambda j: (j, 0)),
        ],
        out_specs=(
            pl.BlockSpec((block, WIDTH), lambda j: (j, 0)),
            pl.BlockSpec((part, WIDTH), lambda j: (j, 0)),
        ),
        scratch_shapes=[
            pltpu.VMEM((OWNERS * PIECES, 128), F32),
            pltpu.VMEM((CAP * OWNERS, WIDTH), BF),
        ],
        compiler_params=pltpu.CompilerParams(vmem_limit_bytes=VMEM_LIMIT),
        name="sums",
    )(wanted, arrived, layer_out)


def local(item_ids, history_len, row_place, item_table, input_proj, output_proj, out_cotangent):
    stored = row_place.at[item_ids[0]].get(mode="promise_in_bounds")
    layer_out, arrived, wanted = layer(
        stored, history_len, item_table, input_proj, output_proj, out_cotangent[0]
    )
    table_grad, layer_out = sum_rows(wanted, arrived, layer_out, item_table.shape[0])
    return layer_out[None], table_grad


def solution(mesh):
    placed = (
        P("table", "seq"),
        P("table"),
        P(),
        P(("table", "seq"), None),
        P(),
        P(),
        P("table", "seq", None),
    )
    return jax.shard_map(
        local,
        mesh=mesh,
        in_specs=placed,
        out_specs=(P("table", "seq", None), P(("table", "seq"), None)),
        check_vma=False,
    )
```

```python
import functools

import jax
import jax.numpy as jnp
from jax import lax
from jax.experimental import pallas as pl
from jax.experimental.pallas import tpu as pltpu
from jax.sharding import PartitionSpec as P

HEADS = 8
CAP = 6
EPS = 1e-05
F32 = jnp.float32
BF = jnp.bfloat16
MESH = pl.DeviceIdType.MESH
VM = pl.BlockSpec(memory_space=pltpu.VMEM)
SM = pl.BlockSpec(memory_space=pltpu.SMEM)
TABLE, SEQ = 8, 16
OWNERS = TABLE * SEQ
LEN = 256
HD = 64
WIDTH = 512
PIECES = CAP * WIDTH // 128
CHUNK = 2 * LEN
CHUNKS = SEQ // 2
AHEAD = 3
VMEM_LIMIT = 56 * 2**20


def nn(a, b):
    return lax.dot_general(a, b, (((1,), (0,)), ((), ())), preferred_element_type=F32)


def nt(a, b):
    return lax.dot_general(a, b, (((1,), (1,)), ((), ())), preferred_element_type=F32)


def iota(shape, dim):
    return lax.broadcasted_iota(jnp.int32, shape, dim)


def silu(x):
    u = 0.5 * x
    return u + u * jnp.tanh(u)


def dsilu(x):
    u = 0.5 * x
    th = jnp.tanh(u)
    return (0.5 + 0.5 * th) * (1.0 + u * (1.0 - th))


def normalize(x, axis=1):
    def mean(y):
        return jnp.mean(y, axis=axis, keepdims=True)

    centred = x - mean(x)
    spread = jnp.sqrt(mean(centred * centred) + EPS)
    return centred / spread, spread


def norm_back(gradient, normed, spread, axis=1):
    def mean(y):
        return jnp.mean(y, axis=axis, keepdims=True)

    return (gradient - mean(gradient) - normed * mean(gradient * normed)) / spread


def places():
    t = lax.axis_index("table")
    s = lax.axis_index("seq")
    return t, s


def greet_all():
    t, s = places()
    me = t * SEQ + s
    sem = pltpu.get_barrier_semaphore()

    def body(i, carry):
        d = lax.rem(me + i, OWNERS)
        pl.semaphore_signal(
            sem, inc=1, device_id=(d // SEQ, lax.rem(d, SEQ)), device_id_type=MESH
        )
        return carry

    lax.fori_loop(1, OWNERS, body, 0)


def wait_all():
    pl.semaphore_wait(pltpu.get_barrier_semaphore(), OWNERS - 1)


def remote(src, dst, send_sem, recv_sem, t, s):
    return pltpu.make_async_remote_copy(
        src_ref=src,
        dst_ref=dst,
        send_sem=send_sem,
        recv_sem=recv_sem,
        device_id=(t, s),
        device_id_type=MESH,
    )


def wait_bytes(ref, sem):
    pltpu.make_async_copy(ref, ref, sem).wait()


def unpack_rows(packed_ref, spread_buf, rows_buf):
    spread_buf[...] = packed_ref[...].astype(F32).reshape(OWNERS * PIECES, 128)
    for r in range(CAP):
        for q in range(WIDTH // 128):
            rows_buf[r * OWNERS : (r + 1) * OWNERS, q * 128 : (q + 1) * 128] = spread_buf[
                pl.ds(r * 4 + q, OWNERS, stride=PIECES), :
            ].astype(BF)


def query_block(core, k):
    return 2 * k + lax.rem(k + core, 2)


def query_core(s):
    return lax.rem((s + 1) // 2, 2)


def pack_rows(rows, count, spread_buf, out_ref, first):
    for r in range(CAP):
        for q in range(WIDTH // 128):
            spread_buf[pl.ds(r * 4 + q, count, stride=PIECES), :] = rows[
                r * count : (r + 1) * count, q * 128 : (q + 1) * 128
            ]
    chunk = spread_buf[: count * PIECES, :]
    out_ref[pl.ds(first, count)] = chunk.astype(BF).reshape(count, PIECES, 128)


def layer_kernel(
    ids_ref, len_ref, place_hbm, table_hbm, win_hbm, wo_hbm, cot_hbm,
    out_ref, grads_ref, want_ref,
    place_ref, look, table_ref, win_ref, wo_ref, cot_ref, all_ids, ids2d, acc, outbuf, ans_ref,
    spread_buf, rows_buf, emb, norm_exact, in_spread, pre, gate, mixed_grad,
    qkv_send, qkv_all, key_nat, value_nat, key_t, value_t,
    o_send, o_all, attn_norm, d_send, d_all,
    dkv_acc, dkv_peer, dkv_send, dkv_all, dq_send, dq_all, qd_pad, p_ahead, c_ahead,
    load_sem, sem, qkv_sem, relay_sem, d_sem, peer_sem,
):
    t, s = places()
    me = t * SEQ + s
    core = lax.rem(t, 2)
    plane = t - core
    head_user = s // HEADS
    head = lax.rem(s, HEADS)
    owner_t = plane + head_user
    my_user = core
    my_core = query_core(s)
    my_slot = s // 2
    rows_dev = table_ref.shape[0]

    loads = [
        pltpu.make_async_copy(src, dst, load_sem.at[n])
        for n, (src, dst) in enumerate(
            ((place_hbm, place_ref), (table_hbm, table_ref), (win_hbm, win_ref), (wo_hbm, wo_ref), (cot_hbm, cot_ref))
        )
    ]
    for load in loads:
        load.start()
    greet_all()

    diagonal = iota((LEN, LEN), 0) == iota((LEN, LEN), 1)
    items = jnp.sum(
        jnp.where(diagonal, ids_ref[...].astype(F32), 0.0), axis=1, keepdims=True
    ).astype(jnp.int32)
    line = items // 128
    look[...] = jnp.zeros_like(look)
    loads[0].wait()
    lines = 512

    def look_up(j, carry):
        base = j * lines
        places_blk = place_ref[pl.ds(pl.multiple_of(base, lines), lines), :]
        digits = jnp.concatenate(
            [((places_blk >> (7 * n)) & 127).astype(F32).astype(BF) for n in range(3)], axis=1
        )
        chosen = (line == iota((LEN, lines), 1) + base).astype(F32).astype(BF)
        look[...] += nn(chosen, digits)
        return carry

    lax.fori_loop(0, place_ref.shape[0] // lines, look_up, 0)
    found = look[:, :128] + 128.0 * look[:, 128:256] + 16384.0 * look[:, 256:]
    mine_at = iota((LEN, 128), 1) == lax.rem(items, 128)
    stored_f = jnp.sum(jnp.where(mine_at, found, 0.0), axis=1, keepdims=True)
    stored = stored_f.astype(jnp.int32)
    all_ids[me] = jnp.sum(
        jnp.where(diagonal, stored_f, 0.0), axis=0, keepdims=True
    ).astype(jnp.int32)
    wait_all()

    def send(src, dst, send_sem, recv_sem, tt, ss):
        local = (tt == t) & (ss == s)

        @pl.when(local)
        def _():
            pltpu.make_async_copy(src, dst, recv_sem).start()

        @pl.when(jnp.logical_not(local))
        def _():
            remote(src, dst, send_sem, recv_sem, tt, ss).start()

    def sent(src, send_sem, tt, ss):
        @pl.when(jnp.logical_not((tt == t) & (ss == s)))
        def _():
            wait_bytes(src, send_sem)

    def to_plane(i, carry):
        ss = lax.rem(s + i, SEQ)
        remote(all_ids.at[me], all_ids.at[me], sem.at[10], sem.at[11], t, ss).start()
        return carry

    lax.fori_loop(1, SEQ, to_plane, 0)
    wait_bytes(all_ids.at[pl.ds(0, SEQ - 1)], sem.at[11])
    mine = all_ids.at[pl.ds(t * SEQ, SEQ)]

    def to_column(i, carry):
        tt = lax.rem(t + i, TABLE)
        remote(mine, mine, sem.at[12], sem.at[13], tt, s).start()
        return carry

    lax.fori_loop(1, TABLE, to_column, 0)

    owner = stored // rows_dev
    owned = (iota((LEN, OWNERS), 1) == owner).astype(F32)
    earlier = (iota((LEN, LEN), 1) < iota((LEN, LEN), 0)).astype(BF)
    rank = jnp.sum(nn(earlier, owned.astype(BF)) * owned, axis=1, keepdims=True)
    slot = rank.astype(jnp.int32) * OWNERS + owner
    positions = s * LEN + iota((LEN, 1), 0)
    live = positions < len_ref[0]

    wait_bytes(all_ids.at[pl.ds(0, (TABLE - 1) * SEQ)], sem.at[13])

    def flat(b, carry):
        ids2d[pl.ds(b, 1), :] = all_ids[lax.rem(t * SEQ + b, OWNERS)]
        return carry

    lax.fori_loop(0, OWNERS, flat, 0, unroll=8)
    ids = ids2d[...]
    hit = ids // rows_dev == me
    local_row = lax.rem(ids, rows_dev).astype(F32)
    before = (iota((LEN, LEN), 0) < iota((LEN, LEN), 1)).astype(BF)
    order = nn(hit.astype(BF), before)
    value = jnp.where(hit, local_row + 1.0, 0.0)
    wanted = []
    for r in range(CAP):
        got = jnp.sum(jnp.where(order == r, value, 0.0), axis=1, keepdims=True) - 1.0
        wanted.append(got.astype(jnp.int32))
    lane = iota((OWNERS, OWNERS), 1)
    square = jnp.full((OWNERS, OWNERS), -1.0, F32)
    for r in range(CAP):
        square = jnp.where(lane == r, wanted[r].astype(F32), square)
    want_ref[...] = square.T[:8].astype(jnp.int32)

    block = 512
    parts = 2
    count = OWNERS // parts
    loads[1].wait()

    def send_one(src_ref, dst_ref, dst_at, send_sem, recv_sem, n):
        tt = lax.rem(t + n // SEQ, TABLE)
        ss = lax.rem(s + n, SEQ)
        remote(
            src_ref.at[n // SEQ * SEQ + ss], dst_ref.at[dst_at(tt)], send_sem, recv_sem, tt, ss
        ).start()

    def send_row(n):
        send_one(outbuf, ans_ref, lambda tt: me, sem.at[14], sem.at[15], n)

    steps = rows_dev // block
    each = count // steps
    for part in range(parts):
        low = part * count

        def gather(j, carry, part=part, low=low):
            base = j * block
            table_blk = table_ref[pl.ds(pl.multiple_of(base, block), block), :]
            cols = iota((count, block), 1) + base
            pick_rows = jnp.concatenate(
                [(w[low : low + count] == cols).astype(F32).astype(BF) for w in wanted], axis=0
            )
            if part:
                for n in range(1 if part == 1 else 0, each):
                    send_row(low - count + j * each + n)
            acc[...] += nn(pick_rows, table_blk)
            return carry

        acc[...] = jnp.zeros_like(acc)
        lax.fori_loop(0, steps, gather, 0)
        pack_rows(acc, count, spread_buf, outbuf, low)

    def send_rest(n, carry):
        send_row(OWNERS - count + n)
        return carry

    lax.fori_loop(0, count, send_rest, 0)
    for n in range(1, steps):
        send_row(n * each)
    ans_ref[me] = outbuf[s]
    pick = (iota((LEN, CAP * OWNERS), 1) == slot).astype(F32).astype(BF)
    for load in loads[2:]:
        load.wait()
    cot = jnp.where(live, cot_ref[...].astype(F32), 0.0)
    mixed_grad[...] = nt(wo_ref[...], cot.astype(BF))
    dkv_acc[...] = jnp.zeros_like(dkv_acc)
    qd_pad[...] = jnp.zeros_like(qd_pad)
    wait_bytes(ans_ref.at[pl.ds(0, OWNERS - 1)], sem.at[15])

    unpack_rows(ans_ref, spread_buf, rows_buf)
    embedded = nn(pick, rows_buf[...])
    emb[...] = embedded
    normed, spread = normalize(embedded)
    norm_exact[...] = normed
    in_spread[...] = jnp.broadcast_to(spread, (LEN, 128))
    pre[...] = nn(normed.astype(BF), win_ref[...])
    for g in range(HEADS // 2):
        for part, (first, scale) in enumerate(((2, 0.0625), (3, 1.0), (1, 1.0))):
            low = first * WIDTH + g * 128
            act = silu(pre[:, low : low + 128]).astype(BF).astype(F32) * scale
            turned = act.T.astype(BF)
            qkv_send[2 * g, part * HD : (part + 1) * HD, :] = turned[:HD]
            qkv_send[2 * g + 1, part * HD : (part + 1) * HD, :] = turned[HD:]

    def send_qkv(i, carry):
        h = lax.rem(i + s, HEADS)
        send(
            qkv_send.at[h], qkv_all.at[s], sem.at[0], qkv_sem.at[my_slot],
            plane + my_core, my_user * HEADS + h,
        )
        return carry

    lax.fori_loop(0, HEADS, send_qkv, 0)

    gate[...] = silu(pre[:, :WIDTH]).T
    pre[...] = dsilu(pre[...])

    peer = plane + 1 - core

    def relay(k):
        i = query_block(core, k)
        wait_bytes(qkv_all.at[i], qkv_sem.at[k])
        ref = qkv_all.at[i, pl.ds(HD, 2 * HD)]
        remote(ref, ref, sem.at[1], relay_sem.at[k], peer, s).start()

    for k in range(AHEAD):
        relay(k)

    def may_see(k):
        offset = lax.rem(k + core, 2) * LEN
        return iota((CHUNK, LEN), 0) <= iota((CHUNK, LEN), 1) + offset

    for k in range(CHUNKS):
        if k + AHEAD < CHUNKS:
            relay(k + AHEAD)
        wait_bytes(qkv_all.at[0, pl.ds(HD, 2 * HD)], relay_sem.at[k])
        for half in range(2):
            both = qkv_all[2 * k + half]
            rows = slice(half * LEN, (half + 1) * LEN)
            key_t[k, :, rows] = both[HD : 2 * HD]
            value_t[k, :, rows] = both[2 * HD :]
            key_nat[k, rows, :] = both[HD : 2 * HD].T
            value_nat[k, rows, :] = both[2 * HD :].T
        query = qkv_all[query_block(core, k), :HD]
        total = None
        for j in range(k + 1):
            u = nn(key_nat[j], query)
            if j == k:
                u = jnp.where(may_see(k), u, 0.0)
            part = nn(value_t[j], (u + u * jnp.tanh(u)).astype(BF))
            total = part if total is None else total + part
        o_send[k] = total
        send(
            o_send.at[k], o_all.at[head], sem.at[2], sem.at[3],
            owner_t, query_block(core, k),
        )

    def score_terms(k, j):
        u = nn(key_nat[j], qkv_all[query_block(core, k), :HD])
        th = jnp.tanh(u)
        a = 1.0 + th
        p = u * a
        c = a * (1.0 + u * (1.0 - th))
        if j == k:
            p = jnp.where(may_see(k), p, 0.0)
            c = jnp.where(may_see(k), c, 0.0)
        return p.astype(BF), c

    def score_ahead(k):
        for j in range(k + 1):
            p, c = score_terms(k, j)
            p_ahead[CHUNKS - 1 - k, j] = p
            c_ahead[CHUNKS - 1 - k, j] = c

    score_ahead(CHUNKS - 1)

    wait_bytes(o_all, sem.at[3])
    attention = o_all[...].reshape(WIDTH, LEN)
    live_lanes = s * LEN + iota((1, LEN), 1) < len_ref[0]
    attention = jnp.where(live_lanes, attention, 0.0)
    attn, attn_spread = normalize(attention, 0)
    attn_norm[...] = attn
    dz = mixed_grad[...] * gate[...]
    attention_grad = norm_back(dz, attn, attn_spread, 0).astype(BF).astype(F32)
    d_send[...] = (0.5 * attention_grad).astype(BF).reshape(HEADS, HD, LEN)

    def send_d(i, carry):
        h = lax.rem(i + s, HEADS)
        send(
            d_send.at[h], d_all.at[my_slot], sem.at[4], d_sem.at[my_slot],
            plane + my_core, my_user * HEADS + h,
        )
        return carry

    lax.fori_loop(0, HEADS, send_d, 0)
    mixed = (attn_norm[...] * gate[...]).T.astype(BF)
    branch = nn(mixed, wo_ref[...])
    out_ref[...] = jnp.where(live, emb[...] + branch, 0.0).astype(BF)

    score_ahead(CHUNKS - 2)

    def reduce_keys(k):
        wait_bytes(dkv_peer.at[k], peer_sem.at[k])
        half = lax.rem(k + core, 2)
        own = dkv_acc[k, pl.ds(pl.multiple_of(half * LEN, LEN), LEN), :]
        dkv_send[k] = (2.0 * (own + dkv_peer[k])).astype(BF)
        send(
            dkv_send.at[k], dkv_all.at[head], sem.at[5], sem.at[6],
            owner_t, query_block(core, k),
        )

    def peer_half(k):
        half = 1 - lax.rem(k + core, 2)
        return dkv_acc.at[k, pl.ds(pl.multiple_of(half * LEN, LEN), LEN)]

    for k in range(CHUNKS - 1, -1, -1):
        wait_bytes(d_all.at[k], d_sem.at[k])
        query = qkv_all[query_block(core, k), :HD]
        grad = d_all[k]
        qd_pad[:LEN, :HD] = query.T
        qd_pad[LEN:, HD:] = grad.T
        pair = qd_pad[...]
        total = None
        for j in range(k + 1):
            if k >= CHUNKS - 2:
                p, c = p_ahead[CHUNKS - 1 - k, j], c_ahead[CHUNKS - 1 - k, j]
            else:
                p, c = score_terms(k, j)
            ds = (nn(value_nat[j], grad) * c).astype(BF)
            dkv_acc[j] += nn(ds, pair[:LEN]) + nn(p, pair[LEN:])
            part = nn(key_t[j], ds)
            total = part if total is None else total + part
        dq_send[k] = (0.125 * total).astype(BF)
        send(
            dq_send.at[k], dq_all.at[head], sem.at[7], sem.at[8],
            owner_t, query_block(core, k),
        )
        remote(peer_half(k), dkv_peer.at[k], sem.at[9], peer_sem.at[k], peer, s).start()
        if k < CHUNKS - 1:
            reduce_keys(k + 1)
    reduce_keys(0)

    def back(first, gradient):
        cols = slice(first * WIDTH, (first + 1) * WIDTH)
        return nt((gradient * pre[:, cols]).astype(BF), win_ref[:, cols])

    def by_head(low):
        return jnp.concatenate(
            [dkv_all[h][:, low : low + HD].astype(F32) for h in range(HEADS)], axis=1
        )

    norm_grad = back(0, (mixed_grad[...] * attn_norm[...]).T)
    wait_bytes(dq_all, sem.at[8])
    norm_grad += back(2, dq_all[...].reshape(WIDTH, LEN).astype(F32).T)
    wait_bytes(dkv_all, sem.at[6])
    norm_grad += back(1, by_head(HD))
    norm_grad += back(3, by_head(0))
    cot = jnp.where(live, cot_ref[...].astype(F32), 0.0)
    embed_grad = cot + norm_back(norm_grad, norm_exact[...], in_spread[:, :1])
    wait_bytes(outbuf.at[pl.ds(0, OWNERS - 1)], sem.at[14])
    turned_owner = lax.rem(owner + (OWNERS - t * SEQ), OWNERS)
    some = CAP * count
    turned_slot = (
        turned_owner // count * some
        + rank.astype(jnp.int32) * count
        + lax.rem(turned_owner, count)
    )
    embed_grad = embed_grad.astype(BF)

    def send_grad(n):
        send_one(
            outbuf, grads_ref, lambda tt: lax.rem(t - tt + TABLE, TABLE) * SEQ + s,
            sem.at[16], sem.at[17], n,
        )

    for part in range(parts):
        chosen = (iota((LEN, some), 1) + part * some == turned_slot).astype(F32).astype(BF)
        put = lax.dot_general(
            chosen, embed_grad, (((0,), (0,)), ((), ())), preferred_element_type=F32
        )
        if part:
            for n in range(1, count):
                send_grad((part - 1) * count + n)
        pack_rows(put, count, spread_buf, outbuf, part * count)
    for part in range(1, parts - 1):
        send_grad(part * count)

    def send_last(n, carry):
        send_grad(OWNERS - count + n)
        return carry

    lax.fori_loop(0, count, send_last, 0)
    grads_ref[s] = outbuf[s]

    wait_bytes(all_ids.at[pl.ds(0, SEQ - 1)], sem.at[10])
    wait_bytes(all_ids.at[pl.ds(0, (TABLE - 1) * SEQ)], sem.at[12])

    def drain(i, carry):
        sent(qkv_send.at[0], sem.at[0], plane + my_core, my_user * HEADS + i)
        sent(d_send.at[0], sem.at[4], plane + my_core, my_user * HEADS + i)
        wait_bytes(qkv_all.at[0, pl.ds(HD, 2 * HD)], sem.at[1])
        wait_bytes(dkv_peer.at[0], sem.at[9])
        block_now = query_block(core, i)
        sent(o_send.at[0], sem.at[2], owner_t, block_now)
        sent(dkv_send.at[0], sem.at[5], owner_t, block_now)
        sent(dq_send.at[0], sem.at[7], owner_t, block_now)
        return carry

    lax.fori_loop(0, CHUNKS, drain, 0)
    wait_bytes(grads_ref.at[pl.ds(0, OWNERS - 1)], sem.at[17])
    wait_bytes(outbuf.at[pl.ds(0, OWNERS - 1)], sem.at[16])


def layer(item_ids, length, row_place, item_table, input_proj, output_proj, cot):
    anywhere = pl.BlockSpec(memory_space=pl.ANY)
    lines = row_place.reshape(-1, 128)
    return pl.pallas_call(
        layer_kernel,
        out_shape=(
            jax.ShapeDtypeStruct((LEN, WIDTH), BF),
            jax.ShapeDtypeStruct((OWNERS, PIECES, 128), BF),
            jax.ShapeDtypeStruct((8, OWNERS), jnp.int32),
        ),
        in_specs=[VM, SM, anywhere, anywhere, anywhere, anywhere, anywhere],
        out_specs=(VM, VM, VM),
        scratch_shapes=[
            pltpu.VMEM(lines.shape, jnp.int32),
            pltpu.VMEM((LEN, 3 * 128), F32),
            pltpu.VMEM(item_table.shape, BF),
            pltpu.VMEM((WIDTH, 4 * WIDTH), BF),
            pltpu.VMEM((WIDTH, WIDTH), BF),
            pltpu.VMEM((LEN, WIDTH), BF),
            pltpu.VMEM((OWNERS, 1, LEN), jnp.int32),
            pltpu.VMEM((OWNERS, LEN), jnp.int32),
            pltpu.VMEM((CAP * OWNERS // 2, WIDTH), F32),
            pltpu.VMEM((OWNERS, PIECES, 128), BF),
            pltpu.VMEM((OWNERS, PIECES, 128), BF),
            pltpu.VMEM((OWNERS * PIECES, 128), F32),
            pltpu.VMEM((CAP * OWNERS, WIDTH), BF),
            pltpu.VMEM((LEN, WIDTH), F32),
            pltpu.VMEM((LEN, WIDTH), F32),
            pltpu.VMEM((LEN, 128), F32),
            pltpu.VMEM((LEN, 4 * WIDTH), F32),
            pltpu.VMEM((WIDTH, LEN), F32),
            pltpu.VMEM((WIDTH, LEN), F32),
            pltpu.VMEM((HEADS, 3 * HD, LEN), BF),
            pltpu.VMEM((SEQ, 3 * HD, LEN), BF),
            pltpu.VMEM((CHUNKS, CHUNK, HD), BF),
            pltpu.VMEM((CHUNKS, CHUNK, HD), BF),
            pltpu.VMEM((CHUNKS, HD, CHUNK), BF),
            pltpu.VMEM((CHUNKS, HD, CHUNK), BF),
            pltpu.VMEM((CHUNKS, HD, LEN), F32),
            pltpu.VMEM((HEADS, HD, LEN), F32),
            pltpu.VMEM((WIDTH, LEN), F32),
            pltpu.VMEM((HEADS, HD, LEN), BF),
            pltpu.VMEM((CHUNKS, HD, LEN), BF),
            pltpu.VMEM((CHUNKS, CHUNK, 2 * HD), F32),
            pltpu.VMEM((CHUNKS, LEN, 2 * HD), F32),
            pltpu.VMEM((CHUNKS, LEN, 2 * HD), BF),
            pltpu.VMEM((HEADS, LEN, 2 * HD), BF),
            pltpu.VMEM((CHUNKS, HD, LEN), BF),
            pltpu.VMEM((HEADS, HD, LEN), BF),
            pltpu.VMEM((2 * LEN, 2 * HD), BF),
            pltpu.VMEM((2, CHUNKS, CHUNK, LEN), BF),
            pltpu.VMEM((2, CHUNKS, CHUNK, LEN), F32),
            pltpu.SemaphoreType.DMA((5,)),
            pltpu.SemaphoreType.DMA((18,)),
            pltpu.SemaphoreType.DMA((CHUNKS,)),
            pltpu.SemaphoreType.DMA((CHUNKS,)),
            pltpu.SemaphoreType.DMA((CHUNKS,)),
            pltpu.SemaphoreType.DMA((CHUNKS,)),
        ],
        compiler_params=pltpu.CompilerParams(
            collective_id=0, has_side_effects=True, vmem_limit_bytes=VMEM_LIMIT
        ),
        name="layer",
    )(item_ids, length, lines, item_table, input_proj, output_proj, cot)


def sum_kernel(block, want_ref, packed_ref, layer_ref, out_ref, same_ref, spread_buf, rows_buf):
    j = pl.program_id(0)

    @pl.when(j == 0)
    def _():
        unpack_rows(packed_ref, spread_buf, rows_buf)

    same_ref[...] = layer_ref[...]
    rows = iota((block, OWNERS), 0) + j * block
    pick = jnp.concatenate(
        [(want_ref[r : r + 1, :] == rows).astype(F32).astype(BF) for r in range(CAP)], axis=1
    )
    out_ref[...] = nn(pick, rows_buf[...]).astype(BF)


def sum_rows(wanted, arrived, layer_out, rows_dev):
    block = 512
    part = LEN * block // rows_dev
    return pl.pallas_call(
        functools.partial(sum_kernel, block),
        out_shape=(
            jax.ShapeDtypeStruct((rows_dev, WIDTH), BF),
            jax.ShapeDtypeStruct((LEN, WIDTH), BF),
        ),
        grid=(rows_dev // block,),
        in_specs=[
            pl.BlockSpec((8, OWNERS), lambda j: (0, 0)),
            pl.BlockSpec((OWNERS, PIECES, 128), lambda j: (0, 0, 0)),
            pl.BlockSpec((part, WIDTH), lambda j: (j, 0)),
        ],
        out_specs=(
            pl.BlockSpec((block, WIDTH), lambda j: (j, 0)),
            pl.BlockSpec((part, WIDTH), lambda j: (j, 0)),
        ),
        scratch_shapes=[
            pltpu.VMEM((OWNERS * PIECES, 128), F32),
            pltpu.VMEM((CAP * OWNERS, WIDTH), BF),
        ],
        compiler_params=pltpu.CompilerParams(vmem_limit_bytes=VMEM_LIMIT),
        name="sums",
    )(wanted, arrived, layer_out)


def local(item_ids, history_len, row_place, item_table, input_proj, output_proj, out_cotangent):
    layer_out, arrived, wanted = layer(
        item_ids, history_len, row_place, item_table, input_proj, output_proj, out_cotangent[0]
    )
    table_grad, layer_out = sum_rows(wanted, arrived, layer_out, item_table.shape[0])
    return layer_out[None], table_grad


def solution(mesh):
    placed = (
        P("table", "seq"),
        P("table"),
        P(),
        P(("table", "seq"), None),
        P(),
        P(),
        P("table", "seq", None),
    )
    return jax.shard_map(
        local,
        mesh=mesh,
        in_specs=placed,
        out_specs=(P("table", "seq", None), P(("table", "seq"), None)),
        check_vma=False,
    )
```

```python
import functools

import jax
import jax.numpy as jnp
from jax import lax
from jax.experimental import pallas as pl
from jax.experimental.pallas import tpu as pltpu
from jax.sharding import PartitionSpec as P

HEADS = 8
CAP = 6
EPS = 1e-05
F32 = jnp.float32
BF = jnp.bfloat16
MESH = pl.DeviceIdType.MESH
VM = pl.BlockSpec(memory_space=pltpu.VMEM)
SM = pl.BlockSpec(memory_space=pltpu.SMEM)
TABLE, SEQ = 8, 16
OWNERS = TABLE * SEQ
LEN = 256
HD = 64
WIDTH = 512
PIECES = CAP * WIDTH // 128
CHUNK = 2 * LEN
CHUNKS = SEQ // 2
AHEAD = 3
VMEM_LIMIT = 56 * 2**20


def nn(a, b):
    return lax.dot_general(a, b, (((1,), (0,)), ((), ())), preferred_element_type=F32)


def nt(a, b):
    return lax.dot_general(a, b, (((1,), (1,)), ((), ())), preferred_element_type=F32)


def iota(shape, dim):
    return lax.broadcasted_iota(jnp.int32, shape, dim)


def silu(x):
    u = 0.5 * x
    return u + u * jnp.tanh(u)


def dsilu(x):
    u = 0.5 * x
    th = jnp.tanh(u)
    return (0.5 + 0.5 * th) * (1.0 + u * (1.0 - th))


def normalize(x, axis=1):
    def mean(y):
        return jnp.mean(y, axis=axis, keepdims=True)

    centred = x - mean(x)
    spread = jnp.sqrt(mean(centred * centred) + EPS)
    return centred / spread, spread


def norm_back(gradient, normed, spread, axis=1):
    def mean(y):
        return jnp.mean(y, axis=axis, keepdims=True)

    return (gradient - mean(gradient) - normed * mean(gradient * normed)) / spread


def places():
    t = lax.axis_index("table")
    s = lax.axis_index("seq")
    return t, s


def greet_all():
    t, s = places()
    me = t * SEQ + s
    sem = pltpu.get_barrier_semaphore()

    def body(i, carry):
        d = lax.rem(me + i, OWNERS)
        pl.semaphore_signal(
            sem, inc=1, device_id=(d // SEQ, lax.rem(d, SEQ)), device_id_type=MESH
        )
        return carry

    lax.fori_loop(1, OWNERS, body, 0)


def wait_all():
    pl.semaphore_wait(pltpu.get_barrier_semaphore(), OWNERS - 1)


def remote(src, dst, send_sem, recv_sem, t, s):
    return pltpu.make_async_remote_copy(
        src_ref=src,
        dst_ref=dst,
        send_sem=send_sem,
        recv_sem=recv_sem,
        device_id=(t, s),
        device_id_type=MESH,
    )


def wait_bytes(ref, sem):
    pltpu.make_async_copy(ref, ref, sem).wait()


def unpack_rows(packed_ref, spread_buf, rows_buf):
    spread_buf[...] = packed_ref[...].astype(F32).reshape(OWNERS * PIECES, 128)
    for r in range(CAP):
        for q in range(WIDTH // 128):
            rows_buf[r * OWNERS : (r + 1) * OWNERS, q * 128 : (q + 1) * 128] = spread_buf[
                pl.ds(r * 4 + q, OWNERS, stride=PIECES), :
            ].astype(BF)


def query_block(core, k):
    return 2 * k + lax.rem(k + core, 2)


def query_core(s):
    return lax.rem((s + 1) // 2, 2)


def pack_rows(rows, count, spread_buf, out_ref, first):
    for r in range(CAP):
        for q in range(WIDTH // 128):
            spread_buf[pl.ds(r * 4 + q, count, stride=PIECES), :] = rows[
                r * count : (r + 1) * count, q * 128 : (q + 1) * 128
            ]
    chunk = spread_buf[: count * PIECES, :]
    out_ref[pl.ds(first, count)] = chunk.astype(BF).reshape(count, PIECES, 128)


def layer_kernel(
    ids_ref, len_ref, place_hbm, table_hbm, win_hbm, wo_hbm, cot_hbm,
    out_ref, grads_ref, want_ref,
    place_ref, look, table_ref, win_ref, wo_ref, cot_ref, all_ids, ids2d, acc, outbuf, ans_ref,
    spread_buf, rows_buf, emb, norm_exact, in_spread, pre, gate, mixed_grad,
    qkv_send, qkv_all, key_nat, value_nat, key_t, value_t,
    o_send, o_all, attn_norm, d_send, d_all,
    dkv_acc, dkv_peer, dkv_send, dkv_all, dq_send, dq_all, qd_pad, p_ahead, c_ahead,
    load_sem, sem, qkv_sem, relay_sem, d_sem, peer_sem,
):
    t, s = places()
    me = t * SEQ + s
    core = lax.rem(t, 2)
    plane = t - core
    head_user = s // HEADS
    head = lax.rem(s, HEADS)
    owner_t = plane + head_user
    my_user = core
    my_core = query_core(s)
    my_slot = s // 2
    rows_dev = table_ref.shape[0]

    loads = [
        pltpu.make_async_copy(src, dst, load_sem.at[n])
        for n, (src, dst) in enumerate(
            ((place_hbm, place_ref), (table_hbm, table_ref), (win_hbm, win_ref), (wo_hbm, wo_ref), (cot_hbm, cot_ref))
        )
    ]
    for load in loads:
        load.start()
    greet_all()

    diagonal = iota((LEN, LEN), 0) == iota((LEN, LEN), 1)
    items = jnp.sum(
        jnp.where(diagonal, ids_ref[...].astype(F32), 0.0), axis=1, keepdims=True
    ).astype(jnp.int32)
    line = items // 128
    look[...] = jnp.zeros_like(look)
    loads[0].wait()
    lines = 512

    def look_up(j, carry):
        base = j * lines
        places_blk = place_ref[pl.ds(pl.multiple_of(base, lines), lines), :]
        digits = jnp.concatenate(
            [((places_blk >> (7 * n)) & 127).astype(F32).astype(BF) for n in range(3)], axis=1
        )
        chosen = (line == iota((LEN, lines), 1) + base).astype(F32).astype(BF)
        look[...] += nn(chosen, digits)
        return carry

    lax.fori_loop(0, place_ref.shape[0] // lines, look_up, 0)
    found = look[:, :128] + 128.0 * look[:, 128:256] + 16384.0 * look[:, 256:]
    mine_at = iota((LEN, 128), 1) == lax.rem(items, 128)
    stored_f = jnp.sum(jnp.where(mine_at, found, 0.0), axis=1, keepdims=True)
    stored = stored_f.astype(jnp.int32)
    all_ids[me] = jnp.sum(
        jnp.where(diagonal, stored_f, 0.0), axis=0, keepdims=True
    ).astype(jnp.int32)
    wait_all()

    def send(src, dst, send_sem, recv_sem, tt, ss):
        local = (tt == t) & (ss == s)

        @pl.when(local)
        def _():
            pltpu.make_async_copy(src, dst, recv_sem).start()

        @pl.when(jnp.logical_not(local))
        def _():
            remote(src, dst, send_sem, recv_sem, tt, ss).start()

    def sent(src, send_sem, tt, ss):
        @pl.when(jnp.logical_not((tt == t) & (ss == s)))
        def _():
            wait_bytes(src, send_sem)

    def to_plane(i, carry):
        ss = lax.rem(s + i, SEQ)
        remote(all_ids.at[me], all_ids.at[me], sem.at[10], sem.at[11], t, ss).start()
        return carry

    lax.fori_loop(1, SEQ, to_plane, 0)
    wait_bytes(all_ids.at[pl.ds(0, SEQ - 1)], sem.at[11])
    mine = all_ids.at[pl.ds(t * SEQ, SEQ)]

    def to_column(i, carry):
        tt = lax.rem(t + i, TABLE)
        remote(mine, mine, sem.at[12], sem.at[13], tt, s).start()
        return carry

    lax.fori_loop(1, TABLE, to_column, 0)

    owner = stored // rows_dev
    owned = (iota((LEN, OWNERS), 1) == owner).astype(F32)
    earlier = (iota((LEN, LEN), 1) < iota((LEN, LEN), 0)).astype(BF)
    rank = jnp.sum(nn(earlier, owned.astype(BF)) * owned, axis=1, keepdims=True)
    slot = rank.astype(jnp.int32) * OWNERS + owner
    positions = s * LEN + iota((LEN, 1), 0)
    live = positions < len_ref[0]

    wait_bytes(all_ids.at[pl.ds(0, (TABLE - 1) * SEQ)], sem.at[13])

    def flat(b, carry):
        ids2d[pl.ds(b, 1), :] = all_ids[lax.rem(t * SEQ + b, OWNERS)]
        return carry

    lax.fori_loop(0, OWNERS, flat, 0, unroll=8)
    ids = ids2d[...]
    hit = ids // rows_dev == me
    local_row = lax.rem(ids, rows_dev).astype(F32)
    before = (iota((LEN, LEN), 0) < iota((LEN, LEN), 1)).astype(BF)
    order = nn(hit.astype(BF), before)
    value = jnp.where(hit, local_row + 1.0, 0.0)
    wanted = []
    for r in range(CAP):
        got = jnp.sum(jnp.where(order == r, value, 0.0), axis=1, keepdims=True) - 1.0
        wanted.append(got.astype(jnp.int32))
    lane = iota((OWNERS, OWNERS), 1)
    square = jnp.full((OWNERS, OWNERS), -1.0, F32)
    for r in range(CAP):
        square = jnp.where(lane == r, wanted[r].astype(F32), square)
    want_ref[...] = square.T[:8].astype(jnp.int32)

    block = 512
    parts = 2
    count = OWNERS // parts
    loads[1].wait()

    def send_one(src_ref, dst_ref, dst_at, send_sem, recv_sem, n):
        tt = lax.rem(t + n // SEQ, TABLE)
        ss = lax.rem(s + n, SEQ)
        remote(
            src_ref.at[n // SEQ * SEQ + ss], dst_ref.at[dst_at(tt)], send_sem, recv_sem, tt, ss
        ).start()

    def send_row(n):
        send_one(outbuf, ans_ref, lambda tt: me, sem.at[14], sem.at[15], n)

    steps = rows_dev // block
    each = count // steps
    for part in range(parts):
        low = part * count

        def gather(j, carry, part=part, low=low):
            base = j * block
            table_blk = table_ref[pl.ds(pl.multiple_of(base, block), block), :]
            cols = iota((count, block), 1) + base
            pick_rows = jnp.concatenate(
                [(w[low : low + count] == cols).astype(F32).astype(BF) for w in wanted], axis=0
            )
            if part:
                for n in range(1 if part == 1 else 0, each):
                    send_row(low - count + j * each + n)
            acc[...] += nn(pick_rows, table_blk)
            return carry

        acc[...] = jnp.zeros_like(acc)
        lax.fori_loop(0, steps, gather, 0)
        pack_rows(acc, count, spread_buf, outbuf, low)

    def send_rest(n, carry):
        send_row(OWNERS - count + n)
        return carry

    lax.fori_loop(0, count, send_rest, 0)
    for n in range(1, steps):
        send_row(n * each)
    ans_ref[me] = outbuf[s]
    pick = (iota((LEN, CAP * OWNERS), 1) == slot).astype(F32).astype(BF)
    for load in loads[2:]:
        load.wait()
    cot = jnp.where(live, cot_ref[...].astype(F32), 0.0)
    mixed_grad[...] = nt(wo_ref[...], cot.astype(BF))
    dkv_acc[...] = jnp.zeros_like(dkv_acc)
    qd_pad[...] = jnp.zeros_like(qd_pad)
    wait_bytes(ans_ref.at[pl.ds(0, OWNERS - 1)], sem.at[15])

    unpack_rows(ans_ref, spread_buf, rows_buf)
    embedded = nn(pick, rows_buf[...])
    emb[...] = embedded
    normed, spread = normalize(embedded)
    norm_exact[...] = normed
    in_spread[...] = jnp.broadcast_to(spread, (LEN, 128))
    pre[...] = nn(normed.astype(BF), win_ref[...])
    for g in range(HEADS // 2):
        for part, (first, scale) in enumerate(((2, 0.0625), (3, 1.0), (1, 1.0))):
            low = first * WIDTH + g * 128
            act = silu(pre[:, low : low + 128]).astype(BF).astype(F32) * scale
            turned = act.T.astype(BF)
            qkv_send[2 * g, part * HD : (part + 1) * HD, :] = turned[:HD]
            qkv_send[2 * g + 1, part * HD : (part + 1) * HD, :] = turned[HD:]

    def send_qkv(i, carry):
        h = lax.rem(i + s, HEADS)
        send(
            qkv_send.at[h], qkv_all.at[s], sem.at[0], qkv_sem.at[my_slot],
            plane + my_core, my_user * HEADS + h,
        )
        return carry

    lax.fori_loop(0, HEADS, send_qkv, 0)

    gate[...] = silu(pre[:, :WIDTH]).T
    pre[...] = dsilu(pre[...])

    peer = plane + 1 - core

    def relay(k):
        i = query_block(core, k)
        wait_bytes(qkv_all.at[i], qkv_sem.at[k])
        ref = qkv_all.at[i, pl.ds(HD, 2 * HD)]
        remote(ref, ref, sem.at[1], relay_sem.at[k], peer, s).start()

    for k in range(AHEAD):
        relay(k)

    def may_see(k):
        offset = lax.rem(k + core, 2) * LEN
        return iota((CHUNK, LEN), 0) <= iota((CHUNK, LEN), 1) + offset

    for k in range(CHUNKS):
        if k + AHEAD < CHUNKS:
            relay(k + AHEAD)
        wait_bytes(qkv_all.at[0, pl.ds(HD, 2 * HD)], relay_sem.at[k])
        for half in range(2):
            both = qkv_all[2 * k + half]
            rows = slice(half * LEN, (half + 1) * LEN)
            key_t[k, :, rows] = both[HD : 2 * HD]
            value_t[k, :, rows] = both[2 * HD :]
            key_nat[k, rows, :] = both[HD : 2 * HD].T
            value_nat[k, rows, :] = both[2 * HD :].T
        query = qkv_all[query_block(core, k), :HD]
        total = None
        for j in range(k + 1):
            u = nn(key_nat[j], query)
            if j == k:
                u = jnp.where(may_see(k), u, 0.0)
            part = nn(value_t[j], (u + u * jnp.tanh(u)).astype(BF))
            total = part if total is None else total + part
        level = jnp.mean(total, axis=0, keepdims=True)
        o_send[k, :HD, :] = (total - level).astype(BF)
        row = iota((HD // 4, LEN), 0)
        terms = jnp.zeros((HD // 4, LEN), F32)
        for n in range(3):
            term = level.astype(BF).astype(F32)
            terms = jnp.where(row == n, term, terms)
            level = level - term
        o_send[k, HD:, :] = terms.astype(BF)
        send(
            o_send.at[k], o_all.at[head], sem.at[2], sem.at[3],
            owner_t, query_block(core, k),
        )

    def score_terms(k, j):
        u = nn(key_nat[j], qkv_all[query_block(core, k), :HD])
        th = jnp.tanh(u)
        a = 1.0 + th
        p = u * a
        c = a * (1.0 + u * (1.0 - th))
        if j == k:
            p = jnp.where(may_see(k), p, 0.0)
            c = jnp.where(may_see(k), c, 0.0)
        return p.astype(BF), c

    def score_ahead(k):
        for j in range(k + 1):
            p, c = score_terms(k, j)
            p_ahead[CHUNKS - 1 - k, j] = p
            c_ahead[CHUNKS - 1 - k, j] = c

    score_ahead(CHUNKS - 1)

    wait_bytes(o_all, sem.at[3])
    attention = jnp.concatenate(
        [
            o_all[h, :HD].astype(F32) + jnp.sum(o_all[h, HD:].astype(F32), axis=0, keepdims=True)
            for h in range(HEADS)
        ],
        axis=0,
    )
    live_lanes = s * LEN + iota((1, LEN), 1) < len_ref[0]
    attention = jnp.where(live_lanes, attention, 0.0)
    attn, attn_spread = normalize(attention, 0)
    attn_norm[...] = attn
    dz = mixed_grad[...] * gate[...]
    attention_grad = norm_back(dz, attn, attn_spread, 0).astype(BF).astype(F32)
    d_send[...] = (0.5 * attention_grad).astype(BF).reshape(HEADS, HD, LEN)

    def send_d(i, carry):
        h = lax.rem(i + s, HEADS)
        send(
            d_send.at[h], d_all.at[my_slot], sem.at[4], d_sem.at[my_slot],
            plane + my_core, my_user * HEADS + h,
        )
        return carry

    lax.fori_loop(0, HEADS, send_d, 0)
    mixed = (attn_norm[...] * gate[...]).T.astype(BF)
    branch = nn(mixed, wo_ref[...])
    out_ref[...] = jnp.where(live, emb[...] + branch, 0.0).astype(BF)

    score_ahead(CHUNKS - 2)

    def reduce_keys(k):
        wait_bytes(dkv_peer.at[k], peer_sem.at[k])
        half = lax.rem(k + core, 2)
        own = dkv_acc[k, pl.ds(pl.multiple_of(half * LEN, LEN), LEN), :]
        dkv_send[k] = (2.0 * (own + dkv_peer[k])).astype(BF)
        send(
            dkv_send.at[k], dkv_all.at[head], sem.at[5], sem.at[6],
            owner_t, query_block(core, k),
        )

    def peer_half(k):
        half = 1 - lax.rem(k + core, 2)
        return dkv_acc.at[k, pl.ds(pl.multiple_of(half * LEN, LEN), LEN)]

    for k in range(CHUNKS - 1, -1, -1):
        wait_bytes(d_all.at[k], d_sem.at[k])
        query = qkv_all[query_block(core, k), :HD]
        grad = d_all[k]
        qd_pad[:LEN, :HD] = query.T
        qd_pad[LEN:, HD:] = grad.T
        pair = qd_pad[...]
        total = None
        for j in range(k + 1):
            if k >= CHUNKS - 2:
                p, c = p_ahead[CHUNKS - 1 - k, j], c_ahead[CHUNKS - 1 - k, j]
            else:
                p, c = score_terms(k, j)
            ds = (nn(value_nat[j], grad) * c).astype(BF)
            dkv_acc[j] += nn(ds, pair[:LEN]) + nn(p, pair[LEN:])
            part = nn(key_t[j], ds)
            total = part if total is None else total + part
        dq_send[k] = (0.125 * total).astype(BF)
        send(
            dq_send.at[k], dq_all.at[head], sem.at[7], sem.at[8],
            owner_t, query_block(core, k),
        )
        remote(peer_half(k), dkv_peer.at[k], sem.at[9], peer_sem.at[k], peer, s).start()
        if k < CHUNKS - 1:
            reduce_keys(k + 1)
    reduce_keys(0)

    def back(first, gradient):
        cols = slice(first * WIDTH, (first + 1) * WIDTH)
        return nt((gradient * pre[:, cols]).astype(BF), win_ref[:, cols])

    def by_head(low):
        return jnp.concatenate(
            [dkv_all[h][:, low : low + HD].astype(F32) for h in range(HEADS)], axis=1
        )

    norm_grad = back(0, (mixed_grad[...] * attn_norm[...]).T)
    wait_bytes(dq_all, sem.at[8])
    norm_grad += back(2, dq_all[...].reshape(WIDTH, LEN).astype(F32).T)
    wait_bytes(dkv_all, sem.at[6])
    norm_grad += back(1, by_head(HD))
    norm_grad += back(3, by_head(0))
    cot = jnp.where(live, cot_ref[...].astype(F32), 0.0)
    embed_grad = cot + norm_back(norm_grad, norm_exact[...], in_spread[:, :1])
    wait_bytes(outbuf.at[pl.ds(0, OWNERS - 1)], sem.at[14])
    turned_owner = lax.rem(owner + (OWNERS - t * SEQ), OWNERS)
    some = CAP * count
    turned_slot = (
        turned_owner // count * some
        + rank.astype(jnp.int32) * count
        + lax.rem(turned_owner, count)
    )
    embed_grad = embed_grad.astype(BF)

    def send_grad(n):
        send_one(
            outbuf, grads_ref, lambda tt: lax.rem(t - tt + TABLE, TABLE) * SEQ + s,
            sem.at[16], sem.at[17], n,
        )

    for part in range(parts):
        chosen = (iota((LEN, some), 1) + part * some == turned_slot).astype(F32).astype(BF)
        put = lax.dot_general(
            chosen, embed_grad, (((0,), (0,)), ((), ())), preferred_element_type=F32
        )
        if part:
            for n in range(1, count):
                send_grad((part - 1) * count + n)
        pack_rows(put, count, spread_buf, outbuf, part * count)
    for part in range(1, parts - 1):
        send_grad(part * count)

    def send_last(n, carry):
        send_grad(OWNERS - count + n)
        return carry

    lax.fori_loop(0, count, send_last, 0)
    grads_ref[s] = outbuf[s]

    wait_bytes(all_ids.at[pl.ds(0, SEQ - 1)], sem.at[10])
    wait_bytes(all_ids.at[pl.ds(0, (TABLE - 1) * SEQ)], sem.at[12])

    def drain(i, carry):
        sent(qkv_send.at[0], sem.at[0], plane + my_core, my_user * HEADS + i)
        sent(d_send.at[0], sem.at[4], plane + my_core, my_user * HEADS + i)
        wait_bytes(qkv_all.at[0, pl.ds(HD, 2 * HD)], sem.at[1])
        wait_bytes(dkv_peer.at[0], sem.at[9])
        block_now = query_block(core, i)
        sent(o_send.at[0], sem.at[2], owner_t, block_now)
        sent(dkv_send.at[0], sem.at[5], owner_t, block_now)
        sent(dq_send.at[0], sem.at[7], owner_t, block_now)
        return carry

    lax.fori_loop(0, CHUNKS, drain, 0)
    wait_bytes(grads_ref.at[pl.ds(0, OWNERS - 1)], sem.at[17])
    wait_bytes(outbuf.at[pl.ds(0, OWNERS - 1)], sem.at[16])


def layer(item_ids, length, row_place, item_table, input_proj, output_proj, cot):
    anywhere = pl.BlockSpec(memory_space=pl.ANY)
    lines = row_place.reshape(-1, 128)
    return pl.pallas_call(
        layer_kernel,
        out_shape=(
            jax.ShapeDtypeStruct((LEN, WIDTH), BF),
            jax.ShapeDtypeStruct((OWNERS, PIECES, 128), BF),
            jax.ShapeDtypeStruct((8, OWNERS), jnp.int32),
        ),
        in_specs=[VM, SM, anywhere, anywhere, anywhere, anywhere, anywhere],
        out_specs=(VM, VM, VM),
        scratch_shapes=[
            pltpu.VMEM(lines.shape, jnp.int32),
            pltpu.VMEM((LEN, 3 * 128), F32),
            pltpu.VMEM(item_table.shape, BF),
            pltpu.VMEM((WIDTH, 4 * WIDTH), BF),
            pltpu.VMEM((WIDTH, WIDTH), BF),
            pltpu.VMEM((LEN, WIDTH), BF),
            pltpu.VMEM((OWNERS, 1, LEN), jnp.int32),
            pltpu.VMEM((OWNERS, LEN), jnp.int32),
            pltpu.VMEM((CAP * OWNERS // 2, WIDTH), F32),
            pltpu.VMEM((OWNERS, PIECES, 128), BF),
            pltpu.VMEM((OWNERS, PIECES, 128), BF),
            pltpu.VMEM((OWNERS * PIECES, 128), F32),
            pltpu.VMEM((CAP * OWNERS, WIDTH), BF),
            pltpu.VMEM((LEN, WIDTH), F32),
            pltpu.VMEM((LEN, WIDTH), F32),
            pltpu.VMEM((LEN, 128), F32),
            pltpu.VMEM((LEN, 4 * WIDTH), F32),
            pltpu.VMEM((WIDTH, LEN), F32),
            pltpu.VMEM((WIDTH, LEN), F32),
            pltpu.VMEM((HEADS, 3 * HD, LEN), BF),
            pltpu.VMEM((SEQ, 3 * HD, LEN), BF),
            pltpu.VMEM((CHUNKS, CHUNK, HD), BF),
            pltpu.VMEM((CHUNKS, CHUNK, HD), BF),
            pltpu.VMEM((CHUNKS, HD, CHUNK), BF),
            pltpu.VMEM((CHUNKS, HD, CHUNK), BF),
            pltpu.VMEM((CHUNKS, HD + HD // 4, LEN), BF),
            pltpu.VMEM((HEADS, HD + HD // 4, LEN), BF),
            pltpu.VMEM((WIDTH, LEN), F32),
            pltpu.VMEM((HEADS, HD, LEN), BF),
            pltpu.VMEM((CHUNKS, HD, LEN), BF),
            pltpu.VMEM((CHUNKS, CHUNK, 2 * HD), F32),
            pltpu.VMEM((CHUNKS, LEN, 2 * HD), F32),
            pltpu.VMEM((CHUNKS, LEN, 2 * HD), BF),
            pltpu.VMEM((HEADS, LEN, 2 * HD), BF),
            pltpu.VMEM((CHUNKS, HD, LEN), BF),
            pltpu.VMEM((HEADS, HD, LEN), BF),
            pltpu.VMEM((2 * LEN, 2 * HD), BF),
            pltpu.VMEM((2, CHUNKS, CHUNK, LEN), BF),
            pltpu.VMEM((2, CHUNKS, CHUNK, LEN), F32),
            pltpu.SemaphoreType.DMA((5,)),
            pltpu.SemaphoreType.DMA((18,)),
            pltpu.SemaphoreType.DMA((CHUNKS,)),
            pltpu.SemaphoreType.DMA((CHUNKS,)),
            pltpu.SemaphoreType.DMA((CHUNKS,)),
            pltpu.SemaphoreType.DMA((CHUNKS,)),
        ],
        compiler_params=pltpu.CompilerParams(
            collective_id=0, has_side_effects=True, vmem_limit_bytes=VMEM_LIMIT
        ),
        name="layer",
    )(item_ids, length, lines, item_table, input_proj, output_proj, cot)


def sum_kernel(block, want_ref, packed_ref, layer_ref, out_ref, same_ref, spread_buf, rows_buf):
    j = pl.program_id(0)

    @pl.when(j == 0)
    def _():
        unpack_rows(packed_ref, spread_buf, rows_buf)

    same_ref[...] = layer_ref[...]
    rows = iota((block, OWNERS), 0) + j * block
    pick = jnp.concatenate(
        [(want_ref[r : r + 1, :] == rows).astype(F32).astype(BF) for r in range(CAP)], axis=1
    )
    out_ref[...] = nn(pick, rows_buf[...]).astype(BF)


def sum_rows(wanted, arrived, layer_out, rows_dev):
    block = 1024
    part = LEN * block // rows_dev
    return pl.pallas_call(
        functools.partial(sum_kernel, block),
        out_shape=(
            jax.ShapeDtypeStruct((rows_dev, WIDTH), BF),
            jax.ShapeDtypeStruct((LEN, WIDTH), BF),
        ),
        grid=(rows_dev // block,),
        in_specs=[
            pl.BlockSpec((8, OWNERS), lambda j: (0, 0)),
            pl.BlockSpec((OWNERS, PIECES, 128), lambda j: (0, 0, 0)),
            pl.BlockSpec((part, WIDTH), lambda j: (j, 0)),
        ],
        out_specs=(
            pl.BlockSpec((block, WIDTH), lambda j: (j, 0)),
            pl.BlockSpec((part, WIDTH), lambda j: (j, 0)),
        ),
        scratch_shapes=[
            pltpu.VMEM((OWNERS * PIECES, 128), F32),
            pltpu.VMEM((CAP * OWNERS, WIDTH), BF),
        ],
        compiler_params=pltpu.CompilerParams(vmem_limit_bytes=VMEM_LIMIT),
        name="sums",
    )(wanted, arrived, layer_out)


def local(item_ids, history_len, row_place, item_table, input_proj, output_proj, out_cotangent):
    layer_out, arrived, wanted = layer(
        item_ids, history_len, row_place, item_table, input_proj, output_proj, out_cotangent[0]
    )
    table_grad, layer_out = sum_rows(wanted, arrived, layer_out, item_table.shape[0])
    return layer_out[None], table_grad


def solution(mesh):
    placed = (
        P("table", "seq"),
        P("table"),
        P(),
        P(("table", "seq"), None),
        P(),
        P(),
        P("table", "seq", None),
    )
    return jax.shard_map(
        local,
        mesh=mesh,
        in_specs=placed,
        out_specs=(P("table", "seq", None), P(("table", "seq"), None)),
        check_vma=False,
    )
```
